256 devices in a mesh: rep: 16 (over y, x_hi, core), fsdp: 16 (over z, x_lo).
Axes of the slice: x: 4 (x_hi: 2, x_lo: 2; x = x_hi * 2 + x_lo), y: 4, z: 8, core: 2. Of those that a mesh axis runs over, the one named last changes fastest.
Arguments:
- layer_input: bfloat16 [49152, 8192], P(('rep', 'fsdp')), may hold values from -180 to 180
- queries: bfloat16 [49152, 4096], P(('rep', 'fsdp')), may hold values from -5 to 5
- rotated_key_heads: bfloat16 [49152, 512], P(('rep', 'fsdp')), may hold values from -5 to 5
- context_gradient: bfloat16 [49152, 4096], P(('rep', 'fsdp')), may hold values from -90 to 90
- value_weight: bfloat16 [8192, 512], P('fsdp'), may hold values from -0.049718446 to 0.049718446
Outputs:
- value_grad: bfloat16 [8192, 512], P('fsdp')
- input_grad: bfloat16 [49152, 8192], P(('rep', 'fsdp'))
- peaks: float32 [2], replicated
- weight_magnitude: float32 [1], replicated
The draws below stay inside these ranges and needn't reach their ends.
All inputs are finite; a program needn't handle non-finite values.
Results may differ from the reference program's by a relative error of at most 0.03.
Values may be sent and summed in bfloat16 or wider, within the bound.
A program may use at most 128 MiB of HBM per device.

```python
import math
import jax
import jax.numpy as jnp
from jax import lax

D = 8192
HEAD_SIZE = 128
QUERY_HEADS = 32
KEY_VALUE_HEADS = 4
DEVICE_TOKENS = 192
TOKEN_TOTAL = 49152


def spread(key, count, top):
    return jnp.exp(jax.random.uniform(key, (count,), jnp.float32) * math.log(top))


def rising(count):
    return jnp.exp(jnp.arange(count, dtype=jnp.float32) * (math.log(3.0) / count))


def draw_layer_input(key, part):
    key = jax.random.fold_in(key, 11)
    noise_key, row_key, column_key = jax.random.split(key, 3)
    noise_draw = jnp.clip(jax.random.normal(noise_key, (TOKEN_TOTAL, D), jnp.float32), -6.0, 6.0)
    row_scale = spread(row_key, TOKEN_TOTAL, 10.0) * rising(TOKEN_TOTAL)
    column_scale = spread(column_key, D, 10.0)
    return (0.1 * noise_draw * row_scale[:, None] * column_scale[None, :]).astype(jnp.bfloat16)


def draw_context_gradient(key, part):
    key = jax.random.fold_in(key, 12)
    noise_key, row_key, column_key = jax.random.split(key, 3)
    noise_draw = jnp.clip(jax.random.normal(noise_key, (TOKEN_TOTAL, QUERY_HEADS * HEAD_SIZE), jnp.float32), -6.0, 6.0)
    row_scale = spread(row_key, TOKEN_TOTAL, 10.0) * rising(TOKEN_TOTAL)
    column_scale = spread(column_key, QUERY_HEADS * HEAD_SIZE, 10.0)
    return (0.05 * noise_draw * row_scale[:, None] * column_scale[None, :]).astype(jnp.bfloat16)


def draw_queries(key, part):
    key = jax.random.fold_in(key, 21)
    heads_per_group = QUERY_HEADS // KEY_VALUE_HEADS
    array_shape = (TOKEN_TOTAL // DEVICE_TOKENS, DEVICE_TOKENS, KEY_VALUE_HEADS, heads_per_group, HEAD_SIZE)
    matrix_entries = jnp.clip(jax.random.normal(key, array_shape, jnp.float32), -5.0, 5.0)
    return matrix_entries.reshape(TOKEN_TOTAL, QUERY_HEADS * HEAD_SIZE).astype(jnp.bfloat16)


def draw_rotated_key_heads(key, part):
    key = jax.random.fold_in(key, 22)
    array_shape = (TOKEN_TOTAL // DEVICE_TOKENS, DEVICE_TOKENS, KEY_VALUE_HEADS, HEAD_SIZE)
    matrix_entries = jnp.clip(jax.random.normal(key, array_shape, jnp.float32), -5.0, 5.0)
    return matrix_entries.reshape(TOKEN_TOTAL, KEY_VALUE_HEADS * HEAD_SIZE).astype(jnp.bfloat16)


def draw_value_weight(key, part):
    key = jax.random.fold_in(key, 31)
    scale_key, noise_key = jax.random.split(key, 2)
    value_head_width = KEY_VALUE_HEADS * HEAD_SIZE
    factor = jax.random.uniform(scale_key, (), jnp.float32, 0.5, 0.9)
    matrix_entries = jnp.clip(jax.random.normal(noise_key, (D, value_head_width), jnp.float32), -4.5, 4.5) * (factor / math.sqrt(D))
    return matrix_entries.astype(jnp.bfloat16)


def setup_inputs(seed: int = 0) -> dict:
    arg_keys = jax.random.split(jax.random.key(seed), 6)
    layer_input = draw_layer_input(jax.random.fold_in(arg_keys[5], 71), 0)
    queries = draw_queries(jax.random.fold_in(arg_keys[5], 71), 0)
    rotated_key_heads = draw_rotated_key_heads(jax.random.fold_in(arg_keys[5], 71), 0)
    context_gradient = draw_context_gradient(jax.random.fold_in(arg_keys[5], 71), 0)
    value_weight = draw_value_weight(jax.random.fold_in(arg_keys[5], 71), 0)
    return dict(layer_input=layer_input, queries=queries, rotated_key_heads=rotated_key_heads, context_gradient=context_gradient, value_weight=value_weight)


FORWARD_TOP = 448.0
BACKWARD_TOP = 57344.0

def value_cotangent(operands):
    query_row_matrix, key_row_matrix, gradient_rows = operands
    sequence_length = query_row_matrix.shape[0]
    heads_per_group = QUERY_HEADS // KEY_VALUE_HEADS
    query_layout = query_row_matrix.reshape(sequence_length, KEY_VALUE_HEADS, heads_per_group, HEAD_SIZE).astype(jnp.float32)
    key_layout = key_row_matrix.reshape(sequence_length, KEY_VALUE_HEADS, HEAD_SIZE).astype(jnp.float32)
    gradient_view = gradient_rows.reshape(sequence_length, KEY_VALUE_HEADS, heads_per_group, HEAD_SIZE).astype(jnp.float32)
    scores = jnp.einsum('qagd,sad->agqs', query_layout, key_layout) * (1.0 / math.sqrt(HEAD_SIZE))
    position = jnp.arange(sequence_length)
    causal = position[None, :] <= position[:, None]
    scores = jnp.where(causal, scores, -jnp.inf)
    row_peak = lax.optimization_barrier(jnp.max(scores, axis=-1, keepdims=True))
    expo = jnp.exp(scores - row_peak)
    probability = (expo / lax.optimization_barrier(jnp.sum(expo, axis=-1, keepdims=True))).astype(jnp.bfloat16)
    backward_cotangent = jnp.einsum('agqs,qagd->sad', probability.astype(jnp.float32), gradient_view)
    return backward_cotangent.reshape(sequence_length, KEY_VALUE_HEADS * HEAD_SIZE)

def reference(layer_input, queries, rotated_key_heads, context_gradient, value_weight):
    sequences = TOKEN_TOTAL // DEVICE_TOKENS
    value_head_width = KEY_VALUE_HEADS * HEAD_SIZE
    peak_input = jnp.max(jnp.abs(layer_input)).astype(jnp.float32)
    peak_weight = jnp.max(jnp.abs(value_weight)).astype(jnp.float32)
    unit_input = (peak_input + 1e-06) / FORWARD_TOP
    unit_weight = (peak_weight + 1e-06) / FORWARD_TOP
    coded_input = (layer_input.astype(jnp.float32) / unit_input).astype(jnp.bfloat16)
    coded_weight = (value_weight.astype(jnp.float32) / unit_weight).astype(jnp.bfloat16)
    backward_cotangent = lax.map(value_cotangent, (queries.reshape(sequences, DEVICE_TOKENS, QUERY_HEADS * HEAD_SIZE), rotated_key_heads.reshape(sequences, DEVICE_TOKENS, value_head_width), context_gradient.reshape(sequences, DEVICE_TOKENS, QUERY_HEADS * HEAD_SIZE)))
    peak_grad = jnp.max(jnp.abs(backward_cotangent))
    unit_grad = (peak_grad + 1e-06) / BACKWARD_TOP
    coded_grad = (backward_cotangent / unit_grad).astype(jnp.bfloat16)
    input_unit = unit_grad * unit_weight

    def input_rows(gradient_rows):
        product = jnp.dot(gradient_rows, coded_weight.T, preferred_element_type=jnp.float32)
        return (product * input_unit).astype(jnp.bfloat16)
    input_grad = lax.map(input_rows, coded_grad).reshape(TOKEN_TOTAL, D)
    factor = unit_input * unit_grad / sequences

    def accumulate(running, operands):
        product = jnp.dot(operands[0].T, operands[1], preferred_element_type=jnp.float32)
        partial_value = (product * factor).astype(jnp.bfloat16)
        return (running + lax.optimization_barrier(partial_value).astype(jnp.float32), None)
    running, _ = lax.scan(accumulate, jnp.zeros((D, value_head_width), jnp.float32), (coded_input.reshape(sequences, DEVICE_TOKENS, D), coded_grad))
    value_grad = running.astype(jnp.bfloat16)
    peaks = jnp.stack([peak_input, peak_grad])
    weight_magnitude = jnp.reshape(peak_weight, (1,))
    return (value_grad, input_grad, peaks, weight_magnitude)
```

```python
import functools
import math

import jax
import jax.numpy as jnp
from jax import lax
from jax.experimental import pallas as pl
from jax.experimental.pallas import tpu as pltpu
from jax.sharding import PartitionSpec as P

HEAD = 128
QUERY_HEADS = 32
KV_HEADS = 4
PER_KV = QUERY_HEADS // KV_HEADS
T = 192
D = 8192
KV = KV_HEADS * HEAD
FORWARD_TOP = 448.0
BACKWARD_TOP = 57344.0
MESH = pl.DeviceIdType.MESH
F32 = jnp.float32
BF16 = jnp.bfloat16
NX, NY, NZ = 4, 4, 8


def place(x, y, z, c):
    x = lax.rem(x + NX, NX)
    y = lax.rem(y + NY, NY)
    z = lax.rem(z + NZ, NZ)
    c = lax.rem(c, 2)
    return ((y * 2 + x // 2) * 2 + c, z * 2 + lax.rem(x, 2))


LINE = [(dx, dc) for dx in range(NX) for dc in range(2) if (dx, dc) != (0, 0)]
GROUP = [(dx, dy) for dx in (0, 2) for dy in range(NY) if (dx, dy) != (0, 0)]
PARTNERS = sorted(
    set((dx, 0, 0, dc) for dx, dc in LINE)
    | set((0, dy, 0, 0) for dy in range(1, NY))
    | set((0, 0, dz, 0) for dz in range(1, NZ))
    | set((dx, dy, 0, 0) for dx, dy in GROUP)
)


class Ring:
    def __init__(self, plus, minus, take, bufs, send, recv, width):
        self.plus, self.minus, self.take, self.width = plus, minus, take, width
        self.bufs, self.send, self.recv = bufs, send, recv
        self.copies = []

    def go(self, src, slot, to):
        copy = pltpu.make_async_remote_copy(
            src_ref=src, dst_ref=self.bufs.at[slot], send_sem=self.send.at[slot],
            recv_sem=self.recv.at[slot], device_id=to, device_id_type=MESH,
        )
        copy.start()
        self.copies.append(copy)

    def arrived(self, slot):
        pltpu.make_async_copy(self.bufs.at[slot], self.bufs.at[slot], self.recv.at[slot]).wait()

    def first(self, part):
        if part == 0:
            self.go(self.take(0, 2), 0, self.plus)
            self.go(self.take(0, -1), 2, self.minus)
        else:
            self.go(self.take(1, 2), 1, self.minus)
            self.go(self.take(1, 1), 3, self.plus)

    def second(self, part):
        step = 1 if part == 0 else -1
        self.arrived(part)
        mine = self.take(part, step)

        def add(i, _):
            mine[i] = (mine[i].astype(F32) + self.bufs[part, i].astype(F32)).astype(BF16)
            return 0

        lax.fori_loop(0, 4, add, 0)
        self.go(mine, 4 + part, self.plus if part == 0 else self.minus)

    def finish(self, part, put):
        self.arrived(2 + part)
        self.arrived(4 + part)
        mine = self.take(part, 0)

        def add(i, _):
            total = mine[i].astype(F32) + self.bufs[2 + part, i].astype(F32)
            put(4 * part + i, total + self.bufs[4 + part, i].astype(F32))
            return 0

        lax.fori_loop(0, 4, add, 0)

    def drain(self):
        for copy in self.copies:
            copy.wait_send()


def kernel(
    x_hbm, q_hbm, k_hbm, g_hbm, w_hbm,
    value_hbm, grad_hbm, peak_out,
    xh, q_v, k_v, g_v, wfull, cot, coded, coded_t,
    part_v, xbuf1, ybuf2, fin, r1, r2, r3, r4, zrecv, piece, piece_all, vout,
    mine_v, other_v, pk, pk1, pk2, pk3,
    load_sem, xown_sem, xs_sem, xr_sem, wown_sem, ax_s, ax_r, az_s, az_r,
    cot_s, cot_r, p1s, p1r, p2s, p2r, p3s, p3r,
    r1s, r1r, r2s, r2r, r3s, r3r, r4s, r4r, zs, zr, cs, cr, own_o, oth_s, oth_r, v_o, v_s, v_r,
):
    rep, fsdp = lax.axis_index("rep"), lax.axis_index("fsdp")
    c = lax.rem(rep, 2)
    xhi = lax.rem(rep // 2, 2)
    y = rep // 4
    xlo = lax.rem(fsdp, 2)
    z = fsdp // 2
    x = 2 * xhi + xlo
    xot = 1 - xlo

    def at(dx=0, dy=0, dz=0, dc=0):
        return place(x + dx, y + dy, z + dz, c + dc)

    mate = at(dc=1)
    barrier = pltpu.get_barrier_semaphore()
    for partner in PARTNERS:
        pl.semaphore_signal(barrier, inc=1, device_id=at(*partner), device_id_type=MESH)

    loads = [pltpu.make_async_copy(k_hbm, k_v, load_sem.at[8])]
    for a in range(KV_HEADS):
        cols = pl.ds(a * PER_KV * HEAD, PER_KV * HEAD)
        loads.append(pltpu.make_async_copy(q_hbm.at[:, cols], q_v.at[:, cols], load_sem.at[a]))
        loads.append(pltpu.make_async_copy(g_hbm.at[:, cols], g_v.at[:, cols], load_sem.at[4 + a]))
    for copy in loads:
        copy.start()
    w_half = w_hbm.at[pl.ds(pl.multiple_of(c * 256, 256), 256), :]
    w_own = pltpu.make_async_copy(w_half, wfull.at[fsdp], wown_sem)
    w_own.start()

    def half_cols(f, half):
        return x_hbm.at[:, pl.ds(pl.multiple_of(f * 512 + half * 256, 256), 256)]

    def x_own(f):
        return pltpu.make_async_copy(half_cols(f, c), xh.at[f, pl.ds(0, T), :], xown_sem.at[f])

    def x_swap(f):
        return pltpu.make_async_remote_copy(
            src_ref=half_cols(f, 1 - c), dst_ref=xh.at[f, pl.ds(T, T), :], send_sem=xs_sem.at[f],
            recv_sem=xr_sem.at[f], device_id=mate, device_id_type=MESH,
        )

    lax.fori_loop(0, 16, lambda f, _: (x_own(f).start(), 0)[1], 0)

    key_pos = lax.broadcasted_iota(jnp.int32, (T, 2 * T), 0)
    query_pos = lax.broadcasted_iota(jnp.int32, (T, 2 * T), 1)
    keep = key_pos <= jnp.where(query_pos >= T, query_pos - T, query_pos)

    def attention(a):
        if a == 0:
            loads[0].wait()
        loads[1 + 2 * a].wait()
        loads[2 + 2 * a].wait()
        keys = k_v[:, a * HEAD:(a + 1) * HEAD]
        total = jnp.zeros((T, HEAD), F32)
        for pair in range(PER_KV // 2):
            base = (a * PER_KV + 2 * pair) * HEAD
            qs = jnp.concatenate([q_v[:, base:base + HEAD], q_v[:, base + HEAD:base + 2 * HEAD]], axis=0)
            gs = jnp.concatenate([g_v[:, base:base + HEAD], g_v[:, base + HEAD:base + 2 * HEAD]], axis=0)
            scores = lax.dot_general(
                keys, qs, (((1,), (1,)), ((), ())), preferred_element_type=F32
            ) * (1.0 / math.sqrt(HEAD))
            scores = jnp.where(keep, scores, -jnp.inf)
            expo = jnp.exp(scores - jnp.max(scores, axis=0, keepdims=True))
            prob = (expo * (1.0 / jnp.sum(expo, axis=0, keepdims=True))).astype(BF16)
            total += jnp.dot(prob, gs, preferred_element_type=F32)
        cot[0, :, a * HEAD:(a + 1) * HEAD] = total

    attention(0)
    pl.semaphore_wait(barrier, len(PARTNERS))

    ax = []
    for i, dx in enumerate((1, -1)):
        rows = pl.ds(128 * i, 128)
        src = w_hbm.at[pl.ds(pl.multiple_of(c * 256 + 128 * i, 128), 128), :]
        ax.append(pltpu.make_async_remote_copy(
            src_ref=src, dst_ref=wfull.at[fsdp, rows, :], send_sem=ax_s.at[i], recv_sem=ax_r.at[i],
            device_id=at(dx=dx), device_id_type=MESH,
        ))
        ax[-1].start()
    az = {}

    def az_slot(way, d, p):
        return (way * 4 + d - 1) * 2 + p

    def az_send(d, p):
        for way, dz in enumerate((1, -1)):
            if d == 4 and p != way:
                continue
            block = lax.rem(z - dz * (d - 1) + NZ, NZ) * 2 + (xlo if p == 0 else xot)
            slot = az_slot(way, d, p)
            src = w_half if d == 1 and p == 0 else wfull.at[block]
            copy = pltpu.make_async_remote_copy(
                src_ref=src, dst_ref=wfull.at[block], send_sem=az_s.at[slot], recv_sem=az_r.at[slot],
                device_id=at(dz=dz), device_id_type=MESH,
            )
            copy.start()
            az[slot] = copy

    def az_wait(d, p):
        for way in range(2):
            if d == 4 and p != way:
                continue
            slot = az_slot(way, d, p)
            pltpu.make_async_copy(wfull.at[0], wfull.at[0], az_r.at[slot]).wait()

    az_send(1, 0)
    lax.fori_loop(0, 16, lambda f, _: (x_swap(f).start(), 0)[1], 0)
    attention(1)
    for i in range(2):
        ax[i].wait_recv()
    az_send(1, 1)
    attention(2)
    attention(3)

    cot_copy = pltpu.make_async_remote_copy(
        src_ref=cot.at[0], dst_ref=cot.at[1], send_sem=cot_s, recv_sem=cot_r,
        device_id=mate, device_id_type=MESH,
    )
    cot_copy.start()

    def x_max(f, top):
        x_own(f).wait()
        x_swap(f).wait_recv()
        return jnp.maximum(top, jnp.max(jnp.abs(xh[f].astype(F32)), axis=0, keepdims=True))

    top_x = lax.fori_loop(0, 16, x_max, jnp.zeros((1, 256), F32))
    top_x = jnp.max(top_x, axis=1, keepdims=True)
    w_own.wait()
    top_w = jnp.max(jnp.max(jnp.abs(wfull[fsdp].astype(F32)), axis=0, keepdims=True), axis=1, keepdims=True)
    top_g = jnp.max(jnp.max(jnp.abs(cot[0]), axis=0, keepdims=True), axis=1, keepdims=True)
    row = lax.broadcasted_iota(jnp.int32, (8, 128), 0)
    pk[0] = jnp.where(row == 0, top_x, jnp.where(row == 1, top_w, top_g))

    pk_copies = []

    def peak_stage(stage, targets, got, s_sem, r_sem):
        for i, to in enumerate(targets):
            copy = pltpu.make_async_remote_copy(
                src_ref=pk.at[stage], dst_ref=got.at[i], send_sem=s_sem.at[i], recv_sem=r_sem.at[i],
                device_id=to, device_id_type=MESH,
            )
            copy.start()
            pk_copies.append(copy)

    def peak_join(stage, count, got, r_sem):
        top = pk[stage]
        for i in range(count):
            pltpu.make_async_copy(got.at[i], got.at[i], r_sem.at[i]).wait()
            top = jnp.maximum(top, got[i])
        pk[stage + 1] = top

    peak_stage(0, [at(dx=dx, dc=dc) for dx, dc in LINE], pk1, p1s, p1r)
    az_wait(1, 0)
    az_send(2, 0)
    peak_join(0, len(LINE), pk1, p1r)
    peak_stage(1, [at(dy=dy) for dy in range(1, NY)], pk2, p2s, p2r)
    peak_join(1, NY - 1, pk2, p2r)
    peak_stage(2, [at(dz=dz) for dz in range(1, NZ)], pk3, p3s, p3r)
    cot_copy.wait_recv()
    peak_join(2, NZ - 1, pk3, p3r)
    az_wait(1, 1)
    az_send(2, 1)
    top = pk[3]
    peak_out[...] = top
    unit_x = (top[0:1, 0:1] + 1e-06) / FORWARD_TOP
    unit_w = (top[1:2, 0:1] + 1e-06) / FORWARD_TOP
    unit_g = (top[2:3, 0:1] + 1e-06) / BACKWARD_TOP
    inv_x, inv_w, inv_g = 1.0 / unit_x, 1.0 / unit_w, 1.0 / unit_g
    input_unit = unit_g * unit_w
    factor = unit_x * unit_g / 256.0
    for i in range(2):
        scaled = cot[i] * inv_g
        coded[pl.ds(T * i, T), :] = scaled.astype(BF16)
    coded_t[...] = jnp.transpose(coded[...].astype(F32)).astype(BF16)

    def product(zd, _):
        for xl in range(2):
            block = (xh[zd * 2 + xl].astype(F32) * inv_x).astype(BF16)
            out = jnp.dot(coded_t[...], block, preferred_element_type=F32) * factor
            part_v[zd, xl] = out.astype(BF16).reshape(2, NY, 64, 256)
        return 0

    def xdest(step):
        xd = lax.rem(x + step + NX, NX)
        return lax.rem(xd, 2), xd // 2

    def ydest(step):
        return lax.rem(y + step + NY, NY)

    def take1(p, step):
        xl, xg = xdest(step)
        return part_v.at[pl.ds(4 * p, 4), xl, xg, :, pl.ds(0, 32), :]

    def take2(p, step):
        return part_v.at[pl.ds(4 * p, 4), :, :, ydest(step), pl.ds(32, 32), :]

    def take3(p, step):
        return xbuf1.at[pl.ds(4 * p, 4), ydest(step)]

    def take4(p, step):
        xl, xg = xdest(step)
        return ybuf2.at[pl.ds(4 * p, 4), xl, xg]

    xp, xm, yp, ym = at(dx=1), at(dx=-1), at(dy=1), at(dy=-1)
    ring1 = Ring(xp, xm, take1, r1, r1s, r1r, 1)
    ring2 = Ring(yp, ym, take2, r2, r2s, r2r, 1)
    ring3 = Ring(yp, ym, take3, r3, r3s, r3r, 1)
    ring4 = Ring(xp, xm, take4, r4, r4s, r4r, 1)

    lax.fori_loop(0, 4, product, 0)
    ring1.first(0)
    ring2.first(0)
    lax.fori_loop(4, 8, product, 0)
    ring1.first(1)
    ring2.first(1)

    def own_out(f):
        return pltpu.make_async_copy(
            mine_v.at[f], grad_hbm.at[:, pl.ds(pl.multiple_of(f * 512 + c * 256, 256), 256)], own_o.at[f]
        )

    def mate_out(f):
        return pltpu.make_async_remote_copy(
            src_ref=other_v.at[f],
            dst_ref=grad_hbm.at[:, pl.ds(pl.multiple_of(f * 512 + c * 256, 256), 256)],
            send_sem=oth_s.at[f], recv_sem=oth_r.at[f], device_id=mate, device_id_type=MESH,
        )

    def input_grad(zb):
        zb = lax.rem(zb + NZ, NZ)

        def one(xl, _):
            f = zb * 2 + xl
            block = (wfull[f].astype(F32) * inv_w).astype(BF16)
            out = lax.dot_general(coded[...], block, (((1,), (1,)), ((), ())), preferred_element_type=F32)
            out = (out * input_unit).astype(BF16)
            mine_v[f] = out[0:T]
            other_v[f] = out[T:2 * T]
            own_out(f).start()
            mate_out(f).start()
            return 0

        lax.fori_loop(0, 2, one, 0)

    input_grad(z)
    az_wait(2, 0)
    az_send(3, 0)
    ring1.second(0)
    ring2.second(0)
    ring1.second(1)
    ring2.second(1)
    input_grad(z - 1)
    input_grad(z + 1)
    az_wait(2, 1)
    az_send(3, 1)

    def put1(i, v):
        xbuf1[i] = v.astype(BF16)

    def put2(i, v):
        ybuf2[i] = v.astype(BF16)

    def put3(i, v):
        fin[i, pl.ds(0, 32), :] = v.astype(BF16)

    def put4(i, v):
        fin[i, pl.ds(32, 32), :] = v.astype(BF16)

    ring1.finish(0, put1)
    ring3.first(0)
    ring2.finish(0, put2)
    ring4.first(0)
    ring1.finish(1, put1)
    ring3.first(1)
    ring2.finish(1, put2)
    ring4.first(1)
    input_grad(z - 2)
    input_grad(z + 2)
    ring3.second(0)
    ring4.second(0)
    ring3.second(1)
    ring4.second(1)
    az_wait(3, 0)
    az_send(4, 0)
    ring3.finish(0, put3)
    ring4.finish(0, put4)
    ring3.finish(1, put3)
    ring4.finish(1, put4)

    z_copies = []
    for i in range(1, NZ):
        zd = lax.rem(z + i, NZ)
        copy = pltpu.make_async_remote_copy(
            src_ref=fin.at[zd], dst_ref=zrecv.at[i], send_sem=zs.at[i], recv_sem=zr.at[i],
            device_id=at(dz=i), device_id_type=MESH,
        )
        copy.start()
        z_copies.append(copy)
    az_wait(3, 1)
    az_send(4, 1)
    input_grad(z - 3)
    input_grad(z + 3)
    total = fin[z].astype(F32)
    for i in range(1, NZ):
        z_copies[i - 1].wait_recv()
        total += zrecv[i].astype(F32)
    j = xhi * NY + y
    piece[...] = total.astype(BF16)

    rows_j = pl.ds(pl.multiple_of(j * 64, 64), 64)
    c_copies = []
    for i, (dx, dy) in enumerate(GROUP):
        copy = pltpu.make_async_remote_copy(
            src_ref=piece, dst_ref=piece_all.at[rows_j, :], send_sem=cs.at[i], recv_sem=cr.at[i],
            device_id=at(dx=dx, dy=dy), device_id_type=MESH,
        )
        copy.start()
        c_copies.append(copy)
    piece_all[rows_j, :] = piece[...]
    az_wait(4, 0)
    az_wait(4, 1)
    input_grad(z + 4)
    for copy in c_copies:
        copy.wait_recv()
    vout[...] = jnp.transpose(piece_all[...].astype(F32)).astype(BF16)
    v_rows = value_hbm.at[pl.ds(pl.multiple_of(c * 256, 256), 256), :]
    v_mine = pltpu.make_async_copy(vout, v_rows, v_o)
    v_mine.start()
    v_mate = pltpu.make_async_remote_copy(
        src_ref=vout, dst_ref=v_rows, send_sem=v_s, recv_sem=v_r, device_id=mate, device_id_type=MESH,
    )
    v_mate.start()

    for copy in ax:
        copy.wait_send()
    for copy in az.values():
        copy.wait_send()
    for copy in pk_copies + z_copies + c_copies + [cot_copy]:
        copy.wait_send()
    for ring in (ring1, ring2, ring3, ring4):
        ring.drain()

    def last(f, _):
        x_swap(f).wait_send()
        own_out(f).wait()
        mate_out(f).wait()
        return 0

    lax.fori_loop(0, 16, last, 0)
    v_mine.wait()
    v_mate.wait()


def body(layer_input, queries, keys, context_gradient, weight):
    dma = pltpu.SemaphoreType.DMA
    vm = pltpu.VMEM
    anywhere = pl.BlockSpec(memory_space=pl.ANY)
    value_grad, input_grad, peaks = pl.pallas_call(
        kernel,
        out_shape=(
            jax.ShapeDtypeStruct((512, KV), BF16),
            jax.ShapeDtypeStruct((T, D), BF16),
            jax.ShapeDtypeStruct((8, 128), F32),
        ),
        in_specs=[anywhere] * 5,
        out_specs=(anywhere, anywhere, pl.BlockSpec(memory_space=pltpu.VMEM)),
        scratch_shapes=[
            vm((16, 2 * T, 256), BF16), vm((T, 4096), BF16), vm((T, KV), BF16), vm((T, 4096), BF16),
            vm((16, 256, KV), BF16), vm((2, T, KV), F32), vm((2 * T, KV), BF16), vm((KV, 2 * T), BF16),
            vm((NZ, 2, 2, NY, 64, 256), BF16), vm((NZ, NY, 32, 256), BF16), vm((NZ, 2, 2, 32, 256), BF16),
            vm((NZ, 64, 256), BF16),
            vm((6, 4, NY, 32, 256), BF16), vm((6, 4, 2, 2, 32, 256), BF16),
            vm((6, 4, 32, 256), BF16), vm((6, 4, 32, 256), BF16),
            vm((NZ, 64, 256), BF16), vm((64, 256), BF16), vm((KV, 256), BF16), vm((256, KV), BF16),
            vm((16, T, 256), BF16), vm((16, T, 256), BF16),
            vm((4, 8, 128), F32), vm((7, 8, 128), F32), vm((3, 8, 128), F32), vm((7, 8, 128), F32),
            dma((9,)), dma((16,)), dma((16,)), dma((16,)), dma, dma((2,)), dma((2,)), dma((16,)), dma((16,)),
            dma, dma, dma((7,)), dma((7,)), dma((3,)), dma((3,)), dma((7,)), dma((7,)),
            dma((6,)), dma((6,)), dma((6,)), dma((6,)), dma((6,)), dma((6,)), dma((6,)), dma((6,)),
            dma((8,)), dma((8,)), dma((7,)), dma((7,)), dma((16,)), dma((16,)), dma((16,)), dma, dma, dma,
        ],
        compiler_params=pltpu.CompilerParams(
            collective_id=0, has_side_effects=True, vmem_limit_bytes=60 << 20
        ),
        name="value_backward",
    )(layer_input, queries, keys, context_gradient, weight)
    return value_grad, input_grad, jnp.stack([peaks[0, 0], peaks[2, 0]]), peaks[1, 0:1]


def solution(mesh):
    return jax.shard_map(
        body,
        mesh=mesh,
        in_specs=(
            P(("rep", "fsdp"), None),
            P(("rep", "fsdp"), None),
            P(("rep", "fsdp"), None),
            P(("rep", "fsdp"), None),
            P("fsdp", None),
        ),
        out_specs=(P("fsdp", None), P(("rep", "fsdp"), None), P(), P()),
        check_vma=False,
    )
```

```python
import functools
import math

import jax
import jax.numpy as jnp
from jax import lax
from jax.experimental import pallas as pl
from jax.experimental.pallas import tpu as pltpu
from jax.sharding import PartitionSpec as P

HEAD = 128
QUERY_HEADS = 32
KV_HEADS = 4
PER_KV = QUERY_HEADS // KV_HEADS
T = 192
D = 8192
KV = KV_HEADS * HEAD
MESH = pl.DeviceIdType.MESH
F32 = jnp.float32
BF16 = jnp.bfloat16
NX, NY, NZ = 4, 4, 8
CUTS = 8


def place(x, y, z, c):
    x = lax.rem(x + NX, NX)
    y = lax.rem(y + NY, NY)
    z = lax.rem(z + NZ, NZ)
    c = lax.rem(c, 2)
    return ((y * 2 + x // 2) * 2 + c, z * 2 + lax.rem(x, 2))


LINE = [(dx, dc) for dx in range(NX) for dc in range(2) if (dx, dc) != (0, 0)]
GROUP = [(dx, dy) for dx in (0, 2) for dy in range(NY) if (dx, dy) != (0, 0)]
PARTNERS = sorted(
    set((dx, 0, 0, dc) for dx, dc in LINE)
    | set((0, dy, 0, 0) for dy in range(1, NY))
    | set((0, 0, dz, 0) for dz in range(1, NZ))
    | set((dx, dy, 0, 0) for dx, dy in GROUP)
)


class Ring:
    def __init__(self, plus, minus, take, put, bufs, send, recv):
        self.plus, self.minus, self.take, self.put = plus, minus, take, put
        self.bufs, self.send, self.recv = bufs, send, recv
        self.copies = []

    def go(self, src, slot, to):
        copy = pltpu.make_async_remote_copy(
            src_ref=src, dst_ref=self.bufs.at[slot], send_sem=self.send.at[slot],
            recv_sem=self.recv.at[slot], device_id=to, device_id_type=MESH,
        )
        copy.start()
        self.copies.append(copy)

    def arrived(self, slot):
        pltpu.make_async_copy(self.bufs.at[slot], self.bufs.at[slot], self.recv.at[slot]).wait()

    def first(self, part):
        if part == 0:
            self.go(self.take(0, 2), 0, self.plus)
            self.go(self.take(0, -1), 2, self.minus)
        else:
            self.go(self.take(1, 2), 1, self.minus)
            self.go(self.take(1, 1), 3, self.plus)

    def second(self, part):
        step = 1 if part == 0 else -1
        self.arrived(part)
        mine = self.take(part, step)

        def add(i, _):
            mine[i] = (mine[i].astype(F32) + self.bufs[part, i].astype(F32)).astype(BF16)
            return 0

        lax.fori_loop(0, 4, add, 0)
        self.go(mine, 4 + part, self.plus if part == 0 else self.minus)

    def finish(self, part):
        self.arrived(2 + part)
        self.arrived(4 + part)
        mine = self.take(part, 0)

        def add(i, _):
            total = mine[i].astype(F32) + self.bufs[2 + part, i].astype(F32)
            self.put(4 * part + i, total + self.bufs[4 + part, i].astype(F32))
            return 0

        lax.fori_loop(0, 4, add, 0)

    def drain(self):
        for copy in self.copies:
            copy.wait_send()


def kernel(
    x_hbm, q_hbm, k_hbm, g_hbm, w_hbm,
    value_hbm, grad_hbm, peak_out,
    xh, q_v, k_v, g_v, wfull, cot, coded_t,
    part_v, xbuf, ybuf, fin, r1, r2, r3, r4, zrecv, piece, piece_all, vout,
    mine_v, other_v, pk, pk1, pk2, pk3,
    load_sem, xown_sem, xs_sem, xr_sem, wown_sem, ax_s, ax_r, az_s, az_r,
    cot_s, cot_r, p1s, p1r, p2s, p2r, p3s, p3r,
    r1s, r1r, r2s, r2r, r3s, r3r, r4s, r4r, zs, zr, cs, cr, own_o, oth_s, oth_r, v_o, v_s, v_r,
):
    rep, fsdp = lax.axis_index("rep"), lax.axis_index("fsdp")
    c = lax.rem(rep, 2)
    xhi = lax.rem(rep // 2, 2)
    y = rep // 4
    xlo = lax.rem(fsdp, 2)
    z = fsdp // 2
    x = 2 * xhi + xlo
    xot = 1 - xlo

    def at(dx=0, dy=0, dz=0, dc=0):
        return place(x + dx, y + dy, z + dz, c + dc)

    mate = at(dc=1)
    barrier = pltpu.get_barrier_semaphore()
    for partner in PARTNERS:
        pl.semaphore_signal(barrier, inc=1, device_id=at(*partner), device_id_type=MESH)

    loads = [pltpu.make_async_copy(k_hbm, k_v, load_sem.at[8])]
    for a in range(KV_HEADS):
        cols = pl.ds(a * PER_KV * HEAD, PER_KV * HEAD)
        loads.append(pltpu.make_async_copy(q_hbm.at[:, cols], q_v.at[:, cols], load_sem.at[a]))
        loads.append(pltpu.make_async_copy(g_hbm.at[:, cols], g_v.at[:, cols], load_sem.at[4 + a]))
    for copy in loads:
        copy.start()
    w_half = w_hbm.at[pl.ds(pl.multiple_of(c * 256, 256), 256), :]
    w_own = pltpu.make_async_copy(w_half, wfull.at[fsdp], wown_sem)
    w_own.start()

    def half_cols(f, half):
        return x_hbm.at[:, pl.ds(pl.multiple_of(f * 512 + half * 256, 256), 256)]

    def x_own(f):
        return pltpu.make_async_copy(half_cols(f, c), xh.at[f, pl.ds(0, T), :], xown_sem.at[f])

    def x_swap(f):
        return pltpu.make_async_remote_copy(
            src_ref=half_cols(f, 1 - c), dst_ref=xh.at[f, pl.ds(T, T), :], send_sem=xs_sem.at[f],
            recv_sem=xr_sem.at[f], device_id=mate, device_id_type=MESH,
        )

    lax.fori_loop(0, 16, lambda f, _: (x_own(f).start(), 0)[1], 0)

    key_pos = lax.broadcasted_iota(jnp.int32, (T, 2 * T), 0)
    query_pos = lax.broadcasted_iota(jnp.int32, (T, 2 * T), 1)
    keep = key_pos <= jnp.where(query_pos >= T, query_pos - T, query_pos)

    def attention(a):
        if a == 0:
            loads[0].wait()
        loads[1 + 2 * a].wait()
        loads[2 + 2 * a].wait()
        keys = k_v[:, a * HEAD:(a + 1) * HEAD]
        total = jnp.zeros((T, HEAD), F32)
        for pair in range(PER_KV // 2):
            base = (a * PER_KV + 2 * pair) * HEAD
            qs = jnp.concatenate([q_v[:, base:base + HEAD], q_v[:, base + HEAD:base + 2 * HEAD]], axis=0)
            gs = jnp.concatenate([g_v[:, base:base + HEAD], g_v[:, base + HEAD:base + 2 * HEAD]], axis=0)
            scores = lax.dot_general(
                keys, qs, (((1,), (1,)), ((), ())), preferred_element_type=F32
            ) * (1.0 / math.sqrt(HEAD))
            scores = jnp.where(keep, scores, -jnp.inf)
            expo = jnp.exp(scores - jnp.max(scores, axis=0, keepdims=True))
            prob = (expo * (1.0 / jnp.sum(expo, axis=0, keepdims=True))).astype(BF16)
            total += jnp.dot(prob, gs, preferred_element_type=F32)
        cot[0, :, a * HEAD:(a + 1) * HEAD] = total.astype(BF16)
        return jnp.max(jnp.abs(total), axis=0, keepdims=True)

    pl.semaphore_wait(barrier, len(PARTNERS))
    lax.fori_loop(0, 16, lambda f, _: (x_swap(f).start(), 0)[1], 0)

    ax = {}

    def across(b, src, block, rows):
        for i, dx in enumerate((1, -1)):
            for k, base in enumerate(rows):
                part = pl.ds(base + 64 * i, 64)
                slot = (b * 2 + k) * 2 + i
                copy = pltpu.make_async_remote_copy(
                    src_ref=src(base + 64 * i), dst_ref=wfull.at[block, part, :],
                    send_sem=ax_s.at[slot], recv_sem=ax_r.at[slot], device_id=at(dx=dx), device_id_type=MESH,
                )
                copy.start()
                ax[slot] = copy

    def across_wait(b, k):
        for i in range(2):
            pltpu.make_async_copy(
                wfull.at[0, pl.ds(0, 64), :], wfull.at[0, pl.ds(0, 64), :], ax_r.at[(b * 2 + k) * 2 + i]
            ).wait()

    def own_rows(base):
        return w_hbm.at[pl.ds(pl.multiple_of(c * 256 + base, 64), 64), :]

    def spread(dz):
        block = lax.rem(z + dz + NZ, NZ) * 2 + xlo
        across(1 + dz % NZ, lambda base: wfull.at[block, pl.ds(base, 64), :], block, (0,))

    az = {}
    WHOLE, LATE, FIRST, LAST = (0, 256), (128, 128), (0, 192), (192, 64)

    def az_list(d, p):
        if d < 4:
            return [(way, 0, WHOLE if p == 0 else LATE) for way in range(2)]
        return [(0, 0, FIRST), (1, 0, LAST)] if p == 0 else [(1, 0, LATE)]

    def az_slot(way, d, p):
        return (way * 4 + d - 1) * 2 + p

    def az_send(d, p):
        for way, _, (base, count) in az_list(d, p):
            dz = 1 - 2 * way
            block = lax.rem(z - dz * (d - 1) + NZ, NZ) * 2 + (xlo if p == 0 else xot)
            slot = az_slot(way, d, p)
            rows = pl.ds(base, count)
            src = w_half if d == 1 and p == 0 else wfull.at[block, rows, :]
            copy = pltpu.make_async_remote_copy(
                src_ref=src, dst_ref=wfull.at[block, rows, :], send_sem=az_s.at[slot], recv_sem=az_r.at[slot],
                device_id=at(dz=dz), device_id_type=MESH,
            )
            copy.start()
            az[slot] = copy

    def az_wait(d, p):
        for way, _, (base, count) in az_list(d, p):
            view = wfull.at[0, pl.ds(base, count), :]
            pltpu.make_async_copy(view, view, az_r.at[az_slot(way, d, p)]).wait()

    cot_copies = []

    def cot_send(s):
        cols = pl.ds(256 * s, 256)
        cot_copies.append(pltpu.make_async_remote_copy(
            src_ref=cot.at[0, :, cols], dst_ref=cot.at[1, :, cols], send_sem=cot_s.at[s], recv_sem=cot_r.at[s],
            device_id=mate, device_id_type=MESH,
        ))
        cot_copies[-1].start()

    pk_copies = []

    def peak_send(stage, targets, got, s_sem, r_sem):
        for i, to in enumerate(targets):
            copy = pltpu.make_async_remote_copy(
                src_ref=pk.at[stage], dst_ref=got.at[i], send_sem=s_sem.at[i], recv_sem=r_sem.at[i],
                device_id=to, device_id_type=MESH,
            )
            copy.start()
            pk_copies.append(copy)

    def peak_join(stage, count, got, r_sem):
        top = pk[stage]
        for i in range(count):
            pltpu.make_async_copy(got.at[i], got.at[i], r_sem.at[i]).wait()
            top = jnp.maximum(top, got[i])
        pk[stage + 1] = top

    def product(s):
        def one(zd, top):
            for xl in range(2):
                f = zd * 2 + xl
                if s == 0:
                    x_own(f).wait()
                    x_swap(f).wait_recv()
                block = xh[f]
                if s == 0:
                    top = jnp.maximum(top, jnp.max(jnp.abs(block.astype(F32)), axis=0, keepdims=True))
                out = jnp.dot(coded_t[...], block, preferred_element_type=F32) * (1.0 / 256.0)
                part_v[s, zd, xl] = out.astype(BF16).reshape(2, 2, NY, 16, 256)
            return top
        return one

    def xdest(step):
        xd = lax.rem(x + step + NX, NX)
        return lax.rem(xd, 2), xd // 2

    def ydest(step):
        return lax.rem(y + step + NY, NY)

    xp, xm, yp, ym = at(dx=1), at(dx=-1), at(dy=1), at(dy=-1)

    def rings(s):
        def take1(p, step):
            xl, xg = xdest(step)
            return part_v.at[s, pl.ds(4 * p, 4), xl, 0, xg]

        def take2(p, step):
            return part_v.at[s, pl.ds(4 * p, 4), :, 1, :, ydest(step)]

        def take3(p, step):
            return xbuf.at[s, pl.ds(4 * p, 4), ydest(step)]

        def take4(p, step):
            xl, xg = xdest(step)
            return ybuf.at[s, pl.ds(4 * p, 4), xl, xg]

        def put1(i, v):
            xbuf[s, i] = v.astype(BF16)

        def put2(i, v):
            ybuf[s, i] = v.astype(BF16)

        def put3(i, v):
            fin[s, i, 0] = v.astype(BF16)

        def put4(i, v):
            fin[s, i, 1] = v.astype(BF16)

        return (
            Ring(xp, xm, take1, put1, r1.at[s], r1s.at[s], r1r.at[s]),
            Ring(yp, ym, take2, put2, r2.at[s], r2s.at[s], r2r.at[s]),
            Ring(yp, ym, take3, put3, r3.at[s], r3s.at[s], r3r.at[s]),
            Ring(xp, xm, take4, put4, r4.at[s], r4s.at[s], r4r.at[s]),
        )

    stages = [rings(0), rings(1)]

    def start(s):
        cot_copies[s].wait_recv()
        both = cot[:, :, 256 * s:256 * (s + 1)].reshape(2 * T, 256)
        coded_t[...] = jnp.transpose(both.astype(F32)).astype(BF16)
        ra, rb = stages[s][:2]
        top = lax.fori_loop(0, 4, product(s), jnp.zeros((1, 256), F32))
        ra.first(0)
        rb.first(0)
        top = lax.fori_loop(4, 8, product(s), top)
        ra.first(1)
        rb.first(1)
        return top

    def second(s, phase):
        ra, rb = stages[s][2 * phase:2 * phase + 2]
        for p in range(2):
            ra.second(p)
            rb.second(p)

    def turn(s):
        for p in range(2):
            for k in range(2):
                stages[s][k].finish(p)
                stages[s][2 + k].first(p)

    z_copies = {}

    def z_send(s):
        for p in range(2):
            for k in range(2):
                stages[s][2 + k].finish(p)
        for i in range(1, NZ):
            zd = lax.rem(z + i, NZ)
            copy = pltpu.make_async_remote_copy(
                src_ref=fin.at[s, zd], dst_ref=zrecv.at[s, i], send_sem=zs.at[s, i], recv_sem=zr.at[s, i],
                device_id=at(dz=i), device_id_type=MESH,
            )
            copy.start()
            z_copies[s, i] = copy

    c_copies = {}
    j = xhi * NY + y

    def c_send(s):
        total = fin[s, z].astype(F32)
        for i in range(1, NZ):
            z_copies[s, i].wait_recv()
            total += zrecv[s, i].astype(F32)
        piece[s] = total.astype(BF16)
        for i, (dx, dy) in enumerate(GROUP):
            copy = pltpu.make_async_remote_copy(
                src_ref=piece.at[s], dst_ref=piece_all.at[pl.ds(2 * s, 2), j], send_sem=cs.at[s, i],
                recv_sem=cr.at[s, i], device_id=at(dx=dx, dy=dy), device_id_type=MESH,
            )
            copy.start()
            c_copies[s, i] = copy
        piece_all[pl.ds(2 * s, 2), j] = piece[s]

    def own_out(f):
        return pltpu.make_async_copy(
            mine_v.at[f], grad_hbm.at[:, pl.ds(pl.multiple_of(f * 512 + c * 256, 256), 256)], own_o.at[f]
        )

    def mate_out(f):
        return pltpu.make_async_remote_copy(
            src_ref=other_v.at[f],
            dst_ref=grad_hbm.at[:, pl.ds(pl.multiple_of(f * 512 + c * 256, 256), 256)],
            send_sem=oth_s.at[f], recv_sem=oth_r.at[f], device_id=mate, device_id_type=MESH,
        )

    def input_grad(zb):
        zb = lax.rem(zb + NZ, NZ)

        def one(xl, _):
            f = zb * 2 + xl
            rows = cot[...].reshape(2 * T, KV)
            out = lax.dot_general(rows, wfull[f], (((1,), (1,)), ((), ())), preferred_element_type=F32)
            out = out.astype(BF16)
            mine_v[f] = out[0:T]
            other_v[f] = out[T:2 * T]
            own_out(f).start()
            mate_out(f).start()
            return 0

        lax.fori_loop(0, 2, one, 0)

    v_copies = []

    def v_send(s):
        for i in range(len(GROUP)):
            c_copies[s, i].wait_recv()
        cols = pl.ds(256 * s, 256)
        turned = jnp.transpose(piece_all[pl.ds(2 * s, 2)].reshape(256, 256).astype(F32))
        vout[:, 256 * s:256 * (s + 1)] = turned.astype(BF16)
        rows = pl.ds(pl.multiple_of(c * 256, 256), 256)
        own = pltpu.make_async_copy(vout.at[:, cols], value_hbm.at[rows, cols], v_o.at[s])
        own.start()
        copy = pltpu.make_async_remote_copy(
            src_ref=vout.at[:, cols], dst_ref=value_hbm.at[rows, cols], send_sem=v_s.at[s], recv_sem=v_r.at[s],
            device_id=mate, device_id_type=MESH,
        )
        copy.start()
        v_copies.extend([own, copy])

    across(0, own_rows, fsdp, (0, 128))
    az_send(1, 0)
    top_g = attention(0)
    top_g = jnp.maximum(top_g, attention(1))
    cot_send(0)
    top_g = jnp.maximum(top_g, attention(2))
    across_wait(0, 1)
    az_send(1, 1)
    top_x = start(0)
    top_g = jnp.maximum(top_g, attention(3))
    cot_send(1)
    second(0, 0)
    start(1)
    w_own.wait()
    top_w = jnp.max(jnp.abs(wfull[fsdp].astype(F32)), axis=0, keepdims=True)
    row = lax.broadcasted_iota(jnp.int32, (8, 128), 0)
    tops = [jnp.max(top, axis=1, keepdims=True) for top in (top_x, top_w, top_g)]
    pk[0] = jnp.where(row == 0, tops[0], jnp.where(row == 1, tops[1], tops[2]))
    peak_send(0, [at(dx=dx, dc=dc) for dx, dc in LINE], pk1, p1s, p1r)
    az_wait(1, 0)
    az_send(2, 0)
    turn(0)
    az_wait(1, 1)
    az_send(2, 1)
    across_wait(0, 0)
    input_grad(z)
    second(1, 0)
    second(0, 1)
    peak_join(0, len(LINE), pk1, p1r)
    peak_send(1, [at(dy=dy) for dy in range(1, NY)], pk2, p2s, p2r)
    az_wait(2, 0)
    az_send(3, 0)
    z_send(0)
    turn(1)
    az_wait(2, 1)
    az_send(3, 1)
    for dz in (1, -1, 2, -2):
        spread(dz)
    peak_join(1, NY - 1, pk2, p2r)
    peak_send(2, [at(dz=dz) for dz in range(1, NZ)], pk3, p3s, p3r)
    second(1, 1)
    c_send(0)
    z_send(1)
    az_wait(3, 0)
    az_send(4, 0)
    spread(3)
    spread(-3)
    for dz in (1, -1):
        across_wait(1 + dz % NZ, 0)
        input_grad(z + dz)
    peak_join(2, NZ - 1, pk3, p3r)
    peak_out[...] = pk[3]
    v_send(0)
    c_send(1)
    az_wait(3, 1)
    az_send(4, 1)
    az_wait(4, 0)
    spread(4)
    for dz in (2, -2, 3, -3):
        across_wait(1 + dz % NZ, 0)
        input_grad(z + dz)
    v_send(1)
    az_wait(4, 1)
    across_wait(1 + 4, 0)
    input_grad(z + 4)

    for copy in ax.values():
        copy.wait_send()
    for copy in az.values():
        copy.wait_send()
    for copy in pk_copies + cot_copies + list(z_copies.values()) + list(c_copies.values()):
        copy.wait_send()
    for ring in stages[0] + stages[1]:
        ring.drain()

    def last(f, _):
        x_swap(f).wait_send()
        own_out(f).wait()
        mate_out(f).wait()
        return 0

    lax.fori_loop(0, 16, last, 0)
    for copy in v_copies:
        copy.wait()


def hand_over(value, grad, peaks, value_out, grad_out, peaks_out, weight_out, value_v, grad_v, come, leave):
    parts = [(value, value_v, value_out)]
    for i in range(CUTS):
        cols = pl.ds(i * (D // CUTS), D // CUTS)
        parts.append((grad.at[:, cols], grad_v.at[:, cols], grad_out.at[:, cols]))
    arrive = [pltpu.make_async_copy(a, b, come.at[i]) for i, (a, b, _) in enumerate(parts)]
    depart = [pltpu.make_async_copy(b, a, leave.at[i]) for i, (_, b, a) in enumerate(parts)]
    for copy in arrive:
        copy.start()
    peaks_out[0] = peaks[0, 0]
    peaks_out[1] = peaks[2, 0]
    weight_out[0] = peaks[1, 0]
    for a, b in zip(arrive, depart):
        a.wait()
        b.start()
    for copy in depart:
        copy.wait()


def body(layer_input, queries, keys, context_gradient, weight):
    dma = pltpu.SemaphoreType.DMA
    vm = pltpu.VMEM
    anywhere = pl.BlockSpec(memory_space=pl.ANY)
    scalars = pl.BlockSpec(memory_space=pltpu.SMEM)
    value_grad, input_grad, peaks = pl.pallas_call(
        kernel,
        out_shape=(
            jax.ShapeDtypeStruct((512, KV), BF16),
            jax.ShapeDtypeStruct((T, D), BF16),
            jax.ShapeDtypeStruct((8, 128), F32),
        ),
        in_specs=[anywhere] * 5,
        out_specs=(anywhere, anywhere, pl.BlockSpec(memory_space=pltpu.VMEM)),
        scratch_shapes=[
            vm((16, 2 * T, 256), BF16), vm((T, 4096), BF16), vm((T, KV), BF16), vm((T, 4096), BF16),
            vm((16, 256, KV), BF16), vm((2, T, KV), BF16), vm((256, 2 * T), BF16),
            vm((2, NZ, 2, 2, 2, NY, 16, 256), BF16), vm((2, NZ, NY, 16, 256), BF16),
            vm((2, NZ, 2, 2, 16, 256), BF16), vm((2, NZ, 2, 16, 256), BF16),
            vm((2, 6, 4, NY, 16, 256), BF16), vm((2, 6, 4, 2, 2, 16, 256), BF16),
            vm((2, 6, 4, 16, 256), BF16), vm((2, 6, 4, 16, 256), BF16),
            vm((2, NZ, 2, 16, 256), BF16), vm((2, 2, 16, 256), BF16), vm((4, 8, 16, 256), BF16),
            vm((256, KV), BF16),
            vm((16, T, 256), BF16), vm((16, T, 256), BF16),
            vm((4, 8, 128), F32), vm((7, 8, 128), F32), vm((3, 8, 128), F32), vm((7, 8, 128), F32),
            dma((9,)), dma((16,)), dma((16,)), dma((16,)), dma, dma((36,)), dma((36,)), dma((16,)), dma((16,)),
            dma((2,)), dma((2,)), dma((7,)), dma((7,)), dma((3,)), dma((3,)), dma((7,)), dma((7,)),
            dma((2, 6)), dma((2, 6)), dma((2, 6)), dma((2, 6)), dma((2, 6)), dma((2, 6)), dma((2, 6)), dma((2, 6)),
            dma((2, 8)), dma((2, 8)), dma((2, 7)), dma((2, 7)), dma((16,)), dma((16,)), dma((16,)), dma((2,)), dma((2,)), dma((2,)),
        ],
        compiler_params=pltpu.CompilerParams(
            collective_id=0, has_side_effects=True, vmem_limit_bytes=60 << 20
        ),
        name="value_backward",
    )(layer_input, queries, keys, context_gradient, weight)
    return pl.pallas_call(
        hand_over,
        out_shape=(
            jax.ShapeDtypeStruct((512, KV), BF16),
            jax.ShapeDtypeStruct((T, D), BF16),
            jax.ShapeDtypeStruct((2,), F32),
            jax.ShapeDtypeStruct((1,), F32),
        ),
        in_specs=[anywhere, anywhere, scalars],
        out_specs=(anywhere, anywhere, scalars, scalars),
        scratch_shapes=[vm((512, KV), BF16), vm((T, D), BF16), dma((1 + CUTS,)), dma((1 + CUTS,))],
        compiler_params=pltpu.CompilerParams(vmem_limit_bytes=60 << 20),
        name="hand_over",
    )(value_grad, input_grad, peaks)


def solution(mesh):
    return jax.shard_map(
        body,
        mesh=mesh,
        in_specs=(
            P(("rep", "fsdp"), None),
            P(("rep", "fsdp"), None),
            P(("rep", "fsdp"), None),
            P(("rep", "fsdp"), None),
            P("fsdp", None),
        ),
        out_specs=(P("fsdp", None), P(("rep", "fsdp"), None), P(), P()),
        check_vma=False,
    )
```

```python
import functools
import math

import jax
import jax.numpy as jnp
from jax import lax
from jax.experimental import pallas as pl
from jax.experimental.pallas import tpu as pltpu
from jax.sharding import PartitionSpec as P

HEAD = 128
QUERY_HEADS = 32
KV_HEADS = 4
PER_KV = QUERY_HEADS // KV_HEADS
T = 192
D = 8192
KV = KV_HEADS * HEAD
MESH = pl.DeviceIdType.MESH
F32 = jnp.float32
BF16 = jnp.bfloat16
NX, NY, NZ = 4, 4, 8
CUTS = 4


def place(x, y, z, c):
    x = lax.rem(x + NX, NX)
    y = lax.rem(y + NY, NY)
    z = lax.rem(z + NZ, NZ)
    c = lax.rem(c, 2)
    return ((y * 2 + x // 2) * 2 + c, z * 2 + lax.rem(x, 2))


class Straight:
    def __init__(self, targets, take, put, bufs, send, recv):
        self.targets, self.take, self.put = targets, take, put
        self.bufs, self.send, self.recv = bufs, send, recv

    def first(self, part):
        for i, to in enumerate(self.targets):
            copy = pltpu.make_async_remote_copy(
                src_ref=self.take(part, i + 1), dst_ref=self.bufs.at[part, i], send_sem=self.send,
                recv_sem=self.recv.at[part], device_id=to, device_id_type=MESH,
            )
            copy.start()

    def finish(self, part):
        landed(self.bufs.at[part], self.recv.at[part])
        mine = self.take(part, 0)

        def add(k, _):
            total = mine[k].astype(F32)
            for i in range(3):
                total += self.bufs[part, i, k].astype(F32)
            self.put(4 * part + k, total)
            return 0

        lax.fori_loop(0, 4, add, 0)

    def drain(self):
        landed(self.bufs, self.send)


LINE = [(dx, dc) for dx in range(NX) for dc in range(2) if (dx, dc) != (0, 0)]
GROUP = [(dx, dy) for dx in (0, 2) for dy in range(NY) if (dx, dy) != (0, 0)]
PARTNERS = sorted(
    set((dx, 0, 0, dc) for dx, dc in LINE)
    | set((0, dy, 0, 0) for dy in range(1, NY))
    | set((0, 0, dz, 0) for dz in range(1, NZ))
    | set((dx, dy, 0, 0) for dx, dy in GROUP)
)


def landed(view, sem):
    pltpu.make_async_copy(view, view, sem).wait()


class Ring:
    def __init__(self, plus, minus, take, put, bufs, send, recv):
        self.plus, self.minus, self.take, self.put = plus, minus, take, put
        self.bufs, self.send, self.recv = bufs, send, recv

    def go(self, src, slot, to):
        copy = pltpu.make_async_remote_copy(
            src_ref=src, dst_ref=self.bufs.at[slot], send_sem=self.send,
            recv_sem=self.recv.at[slot], device_id=to, device_id_type=MESH,
        )
        copy.start()

    def arrived(self, slot):
        landed(self.bufs.at[slot], self.recv.at[slot])

    def first(self, part):
        if part == 0:
            self.go(self.take(0, 2), 0, self.plus)
            self.go(self.take(0, -1), 2, self.minus)
        else:
            self.go(self.take(1, 2), 1, self.minus)
            self.go(self.take(1, 1), 3, self.plus)

    def second(self, part):
        step = 1 if part == 0 else -1
        self.arrived(part)
        mine = self.take(part, step)

        def add(i, _):
            mine[i] = (mine[i].astype(F32) + self.bufs[part, i].astype(F32)).astype(BF16)
            return 0

        lax.fori_loop(0, 4, add, 0)
        self.go(mine, 4 + part, self.plus if part == 0 else self.minus)

    def finish(self, part):
        self.arrived(2 + part)
        self.arrived(4 + part)
        mine = self.take(part, 0)

        def add(i, _):
            total = mine[i].astype(F32) + self.bufs[2 + part, i].astype(F32)
            self.put(4 * part + i, total + self.bufs[4 + part, i].astype(F32))
            return 0

        lax.fori_loop(0, 4, add, 0)

    def drain(self):
        landed(self.bufs, self.send)


def kernel(
    x_hbm, q_hbm, k_hbm, g_hbm, w_hbm,
    value_v, grad_v, peak_out,
    xh, q_v, k_v, g_v, wfull, cot, coded_t,
    part_v, xbuf, ybuf, fin, r1, r2, r3, r4, zrecv, piece, piece_all,
    other_v, pk, pk1, pk2, pk3, x_out,
    load_sem, xown_sem, xother_sem, xs_sem, xr_sem, wown_sem, ax_s, ax_r, az_s, az_r,
    cot_s, cot_r, p1s, p1r, p2s, p2r, p3s, p3r,
    r1s, r1r, r2s, r2r, r3s, r3r, r4s, r4r, zs, zr, cs, cr, oth_s, oth_r, v_s, v_r,
):
    rep, fsdp = lax.axis_index("rep"), lax.axis_index("fsdp")
    c = lax.rem(rep, 2)
    xhi = lax.rem(rep // 2, 2)
    y = rep // 4
    xlo = lax.rem(fsdp, 2)
    z = fsdp // 2
    x = 2 * xhi + xlo
    xot = 1 - xlo

    def at(dx=0, dy=0, dz=0, dc=0):
        return place(x + dx, y + dy, z + dz, c + dc)

    mate = at(dc=1)
    barrier = pltpu.get_barrier_semaphore()
    for partner in PARTNERS:
        pl.semaphore_signal(barrier, inc=1, device_id=at(*partner), device_id_type=MESH)

    def half_cols(f, half):
        return x_hbm.at[:, pl.ds(pl.multiple_of(f * 512 + half * 256, 256), 256)]

    def x_own(f):
        return pltpu.make_async_copy(half_cols(f, c), xh.at[f, pl.ds(0, T), :], xown_sem)

    def x_other(f):
        return pltpu.make_async_copy(half_cols(f, 1 - c), x_out.at[f], xother_sem)

    def x_swap(f):
        return pltpu.make_async_remote_copy(
            src_ref=x_out.at[f], dst_ref=xh.at[f, pl.ds(T, T), :], send_sem=xs_sem,
            recv_sem=xr_sem.at[f // 8], device_id=mate, device_id_type=MESH,
        )

    def x_give(f, _):
        x_swap(f).start()
        return 0


    lax.fori_loop(0, 16, lambda f, _: (x_other(f).start(), 0)[1], 0)
    loads = [pltpu.make_async_copy(k_hbm, k_v, load_sem.at[4])]
    for a in range(KV_HEADS):
        cols = pl.ds(a * PER_KV * HEAD, PER_KV * HEAD)
        loads.append(pltpu.make_async_copy(q_hbm.at[:, cols], q_v.at[:, cols], load_sem.at[a]))
        loads.append(pltpu.make_async_copy(g_hbm.at[:, cols], g_v.at[:, cols], load_sem.at[a]))
    w_half = w_hbm.at[pl.ds(pl.multiple_of(c * 256, 256), 256), :]
    w_own = pltpu.make_async_copy(w_half, wfull.at[fsdp], wown_sem)
    for copy in loads[:5]:
        copy.start()
    w_own.start()
    lax.fori_loop(0, 16, lambda f, _: (x_own(f).start(), 0)[1], 0)
    for copy in loads[5:]:
        copy.start()

    key_pos = lax.broadcasted_iota(jnp.int32, (T, 2 * T), 0)
    query_pos = lax.broadcasted_iota(jnp.int32, (T, 2 * T), 1)
    keep = key_pos <= jnp.where(query_pos >= T, query_pos - T, query_pos)

    def attention(a):
        if a == 0:
            loads[0].wait()
        landed(q_v.at[:, pl.ds(0, 2 * PER_KV * HEAD)], load_sem.at[a])
        keys = k_v[:, a * HEAD:(a + 1) * HEAD]
        total = jnp.zeros((T, HEAD), F32)
        for pair in range(PER_KV // 2):
            base = (a * PER_KV + 2 * pair) * HEAD
            qs = jnp.concatenate([q_v[:, base:base + HEAD], q_v[:, base + HEAD:base + 2 * HEAD]], axis=0)
            gs = jnp.concatenate([g_v[:, base:base + HEAD], g_v[:, base + HEAD:base + 2 * HEAD]], axis=0)
            scores = lax.dot_general(
                keys, qs, (((1,), (1,)), ((), ())), preferred_element_type=F32
            ) * (1.0 / math.sqrt(HEAD))
            scores = jnp.where(keep, scores, -jnp.inf)
            expo = jnp.exp(scores - jnp.max(scores, axis=0, keepdims=True))
            prob = (expo * (1.0 / jnp.sum(expo, axis=0, keepdims=True))).astype(BF16)
            total += jnp.dot(prob, gs, preferred_element_type=F32)
        cot[0, :, a * HEAD:(a + 1) * HEAD] = total.astype(BF16)
        return jnp.max(jnp.abs(total), axis=0, keepdims=True)

    top_g = attention(0)
    pl.semaphore_wait(barrier, len(PARTNERS))
    landed(x_out, xother_sem)
    lax.fori_loop(0, 16, x_give, 0)

    def across(b, src, block, rows):
        for i, dx in enumerate((1, -1)):
            for k, base in enumerate(rows):
                part = pl.ds(base + 64 * i, 64)
                copy = pltpu.make_async_remote_copy(
                    src_ref=src(base + 64 * i), dst_ref=wfull.at[block, part, :],
                    send_sem=ax_s.at[b + 8 * k], recv_sem=ax_r.at[b + 8 * k], device_id=at(dx=dx), device_id_type=MESH,
                )
                copy.start()

    def across_wait(b, k):
        landed(wfull.at[0, pl.ds(0, 128), :], ax_r.at[b + 8 * k])

    def own_rows(base):
        return wfull.at[fsdp, pl.ds(base, 64), :]

    def spread(dz):
        block = lax.rem(z + dz + NZ, NZ) * 2 + xlo
        across(dz % NZ, lambda base: wfull.at[block, pl.ds(base, 64), :], block, (0,))

    WHOLE, LATE, FIRST, LAST = (0, 256), (128, 128), (0, 192), (192, 64)

    def az_list(d, p):
        if d < 4:
            return [(way, 0, WHOLE if p == 0 else LATE) for way in range(2)]
        return [(0, 0, FIRST), (1, 0, LAST)] if p == 0 else [(1, 0, LATE)]

    def az_slot(d, p):
        return (d - 1) * 2 + p

    def az_view(d, p):
        if p == 0 and d < 4:
            return wfull.at[pl.ds(0, 2)]
        return wfull.at[0, pl.ds(0, 128 if p == 1 and d == 4 else 256), :]

    def az_send(d, p):
        for way, _, (base, count) in az_list(d, p):
            dz = 1 - 2 * way
            block = lax.rem(z - dz * (d - 1) + NZ, NZ) * 2 + (xlo if p == 0 else xot)
            slot = az_slot(d, p)
            rows = pl.ds(base, count)
            copy = pltpu.make_async_remote_copy(
                src_ref=wfull.at[block, rows, :], dst_ref=wfull.at[block, rows, :], send_sem=az_s.at[slot], recv_sem=az_r.at[slot],
                device_id=at(dz=dz), device_id_type=MESH,
            )
            copy.start()

    def az_wait(d, p):
        landed(az_view(d, p), az_r.at[az_slot(d, p)])

    cot_copies = []

    def cot_send(s):
        cols = pl.ds(256 * s, 256)
        cot_copies.append(pltpu.make_async_remote_copy(
            src_ref=cot.at[0, :, cols], dst_ref=cot.at[1, :, cols], send_sem=cot_s.at[s], recv_sem=cot_r.at[s],
            device_id=mate, device_id_type=MESH,
        ))
        cot_copies[-1].start()

    def peak_send(stage, targets, got, s_sem, r_sem):
        for i, to in enumerate(targets):
            copy = pltpu.make_async_remote_copy(
                src_ref=pk.at[stage], dst_ref=got.at[i], send_sem=s_sem, recv_sem=r_sem,
                device_id=to, device_id_type=MESH,
            )
            copy.start()

    def peak_join(stage, count, got, r_sem):
        top = pk[stage]
        landed(got, r_sem)
        for i in range(count):
            top = jnp.maximum(top, got[i])
        pk[stage + 1] = top

    def product(s):
        def one(pair, _):
            for k in range(4):
                zd, xl = pair * 2 + k // 2, k % 2
                out = jnp.dot(coded_t[...], xh[zd * 2 + xl], preferred_element_type=F32)
                part_v[s, zd, xl] = out.astype(BF16).reshape(2, 2, NY, 16, 256)
            return 0
        return one

    def xdest(step):
        xd = lax.rem(x + step + NX, NX)
        return lax.rem(xd, 2), xd // 2

    def ydest(step):
        return lax.rem(y + step + NY, NY)

    xp, xm, yp, ym = at(dx=1), at(dx=-1), at(dy=1), at(dy=-1)

    def rings(s):
        def take1(p, step):
            xl, xg = xdest(step)
            return part_v.at[s, pl.ds(4 * p, 4), xl, 0, xg]

        def take2(p, step):
            return part_v.at[s, pl.ds(4 * p, 4), :, 1, :, ydest(step)]

        def take3(p, step):
            return xbuf.at[s, pl.ds(4 * p, 4), ydest(step)]

        def take4(p, step):
            xl, xg = xdest(step)
            return ybuf.at[s, pl.ds(4 * p, 4), xl, xg]

        def put1(i, v):
            xbuf[s, i] = v.astype(BF16)

        def put2(i, v):
            ybuf[s, i] = v.astype(BF16)

        def put3(i, v):
            fin[s, i, 0] = v.astype(BF16)

        def put4(i, v):
            fin[s, i, 1] = v.astype(BF16)

        return (
            Ring(xp, xm, take1, put1, r1.at[s], r1s.at[s], r1r.at[s]),
            Ring(yp, ym, take2, put2, r2.at[s], r2s.at[s], r2r.at[s]),
            Straight([at(dy=i) for i in (1, 2, 3)], take3, put3, r3.at[s], r3s.at[s], r3r.at[s]),
            Straight([at(dx=i) for i in (1, 2, 3)], take4, put4, r4.at[s], r4s.at[s], r4r.at[s]),
        )

    stages = [rings(0), rings(1)]

    def start(s):
        cot_copies[s].wait_recv()
        both = cot[:, :, 256 * s:256 * (s + 1)].reshape(2 * T, 256)
        coded_t[...] = jnp.transpose(both.astype(F32)).astype(BF16)
        ra, rb = stages[s][:2]
        if s == 0:
            landed(x_out, xown_sem)
            landed(x_out.at[pl.ds(0, 8)], xr_sem.at[0])
        lax.fori_loop(0, 2, product(s), 0)
        ra.first(0)
        rb.first(0)
        if s == 0:
            landed(x_out.at[pl.ds(0, 8)], xr_sem.at[1])
        lax.fori_loop(2, 4, product(s), 0)
        ra.first(1)
        rb.first(1)

    def second(s):
        ra, rb = stages[s][:2]
        for p in range(2):
            ra.second(p)
            rb.second(p)

    def turn(s):
        for p in range(2):
            for k in range(2):
                stages[s][k].finish(p)
                stages[s][2 + k].first(p)

    def z_send(s):
        for p in range(2):
            for k in range(2):
                stages[s][2 + k].finish(p)
        for i in range(1, NZ):
            zd = lax.rem(z + i, NZ)
            copy = pltpu.make_async_remote_copy(
                src_ref=fin.at[s, zd], dst_ref=zrecv.at[s, i], send_sem=zs.at[s], recv_sem=zr.at[s],
                device_id=at(dz=i), device_id_type=MESH,
            )
            copy.start()

    j = xhi * NY + y

    def c_send(s):
        total = fin[s, z].astype(F32)
        landed(zrecv.at[s, pl.ds(1, NZ - 1)], zr.at[s])
        for i in range(1, NZ):
            total += zrecv[s, i].astype(F32)
        piece[s] = (total * (1.0 / 256.0)).astype(BF16)
        for i, (dx, dy) in enumerate(GROUP):
            copy = pltpu.make_async_remote_copy(
                src_ref=piece.at[s], dst_ref=piece_all.at[pl.ds(2 * s, 2), j], send_sem=cs.at[s],
                recv_sem=cr.at[s], device_id=at(dx=dx, dy=dy), device_id_type=MESH,
            )
            copy.start()
        piece_all[pl.ds(2 * s, 2), j] = piece[s]

    def out_cols(f):
        return pl.ds(pl.multiple_of(f * 512 + c * 256, 256), 256)

    def mate_out(f):
        return pltpu.make_async_remote_copy(
            src_ref=other_v.at[f], dst_ref=grad_v.at[:, out_cols(f)],
            send_sem=oth_s, recv_sem=oth_r, device_id=mate, device_id_type=MESH,
        )

    def input_grad(zb):
        zb = lax.rem(zb + NZ, NZ)

        rows = cot[...].reshape(2 * T, KV)
        for xl in range(2):
            f = zb * 2 + xl
            out = lax.dot_general(rows, wfull[f], (((1,), (1,)), ((), ())), preferred_element_type=F32)
            out = out.astype(BF16)
            grad_v[:, out_cols(f)] = out[0:T]
            other_v[f] = out[T:2 * T]
        for xl in range(2):
            mate_out(zb * 2 + xl).start()

    v_copies = []

    def v_send(s):
        landed(zrecv.at[s, pl.ds(1, NZ - 1)], cr.at[s])
        cols = pl.ds(256 * s, 256)
        turned = jnp.transpose(piece_all[pl.ds(2 * s, 2)].reshape(256, 256).astype(F32))
        rows = pl.ds(pl.multiple_of(c * 256, 256), 256)
        value_v[rows, cols] = turned.astype(BF16)
        copy = pltpu.make_async_remote_copy(
            src_ref=value_v.at[rows, cols], dst_ref=value_v.at[rows, cols], send_sem=v_s.at[s], recv_sem=v_r.at[s],
            device_id=mate, device_id_type=MESH,
        )
        copy.start()
        v_copies.append(copy)

    w_own.wait()
    across(0, own_rows, fsdp, (0, 128))
    az_send(1, 0)
    top_g = jnp.maximum(top_g, attention(1))
    cot_send(0)
    top_g = jnp.maximum(top_g, attention(2))
    top_g = jnp.maximum(top_g, attention(3))
    cot_send(1)
    start(0)
    across_wait(0, 1)
    az_send(1, 1)
    start(1)
    second(0)
    az_wait(1, 0)
    az_send(2, 0)
    top_x = lax.fori_loop(
        0, 16,
        lambda f, top: jnp.maximum(top, jnp.max(jnp.abs(xh[f].astype(F32)), axis=0, keepdims=True)),
        jnp.zeros((1, 256), F32),
    )
    top_w = jnp.max(jnp.abs(wfull[fsdp].astype(F32)), axis=0, keepdims=True)
    row = lax.broadcasted_iota(jnp.int32, (8, 128), 0)
    tops = [jnp.max(top, axis=1, keepdims=True) for top in (top_x, top_w, top_g)]
    pk[0] = jnp.where(row == 0, tops[0], jnp.where(row == 1, tops[1], tops[2]))
    peak_send(0, [at(dx=dx, dc=dc) for dx, dc in LINE], pk1, p1s, p1r)
    second(1)
    az_wait(1, 1)
    az_send(2, 1)
    turn(0)
    across_wait(0, 0)
    input_grad(z)
    az_wait(2, 0)
    az_send(3, 0)
    turn(1)
    spread(1)
    spread(-1)
    peak_join(0, len(LINE), pk1, p1r)
    peak_send(1, [at(dy=dy) for dy in range(1, NY)], pk2, p2s, p2r)
    az_wait(2, 1)
    az_send(3, 1)
    z_send(0)
    z_send(1)
    spread(2)
    spread(-2)
    az_wait(3, 0)
    az_send(4, 0)
    for dz in (1, -1):
        across_wait(dz % NZ, 0)
        input_grad(z + dz)
    c_send(0)
    az_wait(3, 1)
    az_send(4, 1)
    spread(3)
    spread(-3)
    peak_join(1, NY - 1, pk2, p2r)
    peak_send(2, [at(dz=dz) for dz in range(1, NZ)], pk3, p3s, p3r)
    c_send(1)
    for dz in (2, -2):
        across_wait(dz % NZ, 0)
        input_grad(z + dz)
    az_wait(4, 0)
    spread(4)
    v_send(0)
    for dz in (3, -3):
        across_wait(dz % NZ, 0)
        input_grad(z + dz)
    v_send(1)
    peak_join(2, NZ - 1, pk3, p3r)
    peak_out[...] = pk[3]
    az_wait(4, 1)
    across_wait(4, 0)
    input_grad(z + 4)

    for b in range(9):
        landed(wfull.at[0, pl.ds(0, 128), :], ax_s.at[b])
    for d in range(1, 5):
        for p in range(2):
            landed(az_view(d, p), az_s.at[az_slot(d, p)])
    for got, sem in ((pk1, p1s), (pk2, p2s), (pk3, p3s)):
        landed(got, sem)
    for s in range(2):
        cot_copies[s].wait_send()
        landed(zrecv.at[s, pl.ds(1, NZ - 1)], zs.at[s])
        landed(zrecv.at[s, pl.ds(1, NZ - 1)], cs.at[s])
    for ring in stages[0] + stages[1]:
        ring.drain()

    landed(x_out, xs_sem)
    landed(other_v, oth_s)
    landed(other_v, oth_r)
    for copy in v_copies:
        copy.wait()


def hand_over(value, grad, peaks, value_out, grad_out, peaks_out, weight_out, sems):
    copies = [pltpu.make_async_copy(value, value_out, sems.at[0])]
    for i in range(CUTS):
        rows = pl.ds(i * (T // CUTS), T // CUTS)
        copies.append(pltpu.make_async_copy(grad.at[rows], grad_out.at[rows], sems.at[1 + i]))
    for copy in copies:
        copy.start()
    peaks_out[0] = jnp.max(peaks[0:1])
    peaks_out[1] = jnp.max(peaks[2:3])
    weight_out[0] = jnp.max(peaks[1:2])
    for copy in copies:
        copy.wait()


def body(layer_input, queries, keys, context_gradient, weight):
    dma = pltpu.SemaphoreType.DMA
    vm = pltpu.VMEM
    anywhere = pl.BlockSpec(memory_space=pl.ANY)
    scalars = pl.BlockSpec(memory_space=pltpu.SMEM)
    value_grad, input_grad, peaks = pl.pallas_call(
        kernel,
        out_shape=(
            vm((512, KV), BF16),
            vm((T, D), BF16),
            vm((8, 128), F32),
        ),
        in_specs=[anywhere] * 5,
        out_specs=(pl.BlockSpec(memory_space=pltpu.VMEM),) * 3,
        scratch_shapes=[
            vm((16, 2 * T, 256), BF16), vm((T, 4096), BF16), vm((T, KV), BF16), vm((T, 4096), BF16),
            vm((16, 256, KV), BF16), vm((2, T, KV), BF16), vm((256, 2 * T), BF16),
            vm((2, NZ, 2, 2, 2, NY, 16, 256), BF16), vm((2, NZ, NY, 16, 256), BF16),
            vm((2, NZ, 2, 2, 16, 256), BF16), vm((2, NZ, 2, 16, 256), BF16),
            vm((2, 6, 4, NY, 16, 256), BF16), vm((2, 6, 4, 2, 2, 16, 256), BF16),
            vm((2, 2, 3, 4, 16, 256), BF16), vm((2, 2, 3, 4, 16, 256), BF16),
            vm((2, NZ, 2, 16, 256), BF16), vm((2, 2, 16, 256), BF16), vm((4, 8, 16, 256), BF16),
            vm((16, T, 256), BF16),
            vm((4, 8, 128), F32), vm((7, 8, 128), F32), vm((3, 8, 128), F32), vm((7, 8, 128), F32),
            vm((16, T, 256), BF16),
            dma((5,)), dma, dma, dma, dma((2,)), dma, dma((9,)), dma((9,)), dma((8,)), dma((8,)),
            dma((2,)), dma((2,)), dma, dma, dma, dma, dma, dma,
            dma((2,)), dma((2, 6)), dma((2,)), dma((2, 6)), dma((2,)), dma((2, 2)), dma((2,)), dma((2, 2)),
            dma((2,)), dma((2,)), dma((2,)), dma((2,)), dma, dma, dma((2,)), dma((2,)),
        ],
        compiler_params=pltpu.CompilerParams(
            collective_id=0, has_side_effects=True, vmem_limit_bytes=60 << 20
        ),
        name="value_backward",
    )(layer_input, queries, keys, context_gradient, weight)
    return pl.pallas_call(
        hand_over,
        out_shape=(
            jax.ShapeDtypeStruct((512, KV), BF16),
            jax.ShapeDtypeStruct((T, D), BF16),
            jax.ShapeDtypeStruct((2,), F32),
            jax.ShapeDtypeStruct((1,), F32),
        ),
        in_specs=[pl.BlockSpec(memory_space=pltpu.VMEM)] * 3,
        out_specs=(anywhere, anywhere, scalars, scalars),
        scratch_shapes=[dma((1 + CUTS,))],
        compiler_params=pltpu.CompilerParams(vmem_limit_bytes=1 << 20),
        name="hand_over",
    )(value_grad, input_grad, peaks)


def solution(mesh):
    return jax.shard_map(
        body,
        mesh=mesh,
        in_specs=(
            P(("rep", "fsdp"), None),
            P(("rep", "fsdp"), None),
            P(("rep", "fsdp"), None),
            P(("rep", "fsdp"), None),
            P("fsdp", None),
        ),
        out_specs=(P("fsdp", None), P(("rep", "fsdp"), None), P(), P()),
        check_vma=False,
    )
```

```python
import functools
import math

import jax
import jax.numpy as jnp
from jax import lax
from jax.experimental import pallas as pl
from jax.experimental.pallas import tpu as pltpu
from jax.sharding import PartitionSpec as P

HEAD = 128
QUERY_HEADS = 32
KV_HEADS = 4
PER_KV = QUERY_HEADS // KV_HEADS
T = 192
D = 8192
KV = KV_HEADS * HEAD
MESH = pl.DeviceIdType.MESH
F32 = jnp.float32
BF16 = jnp.bfloat16
NX, NY, NZ = 4, 4, 8
CUTS = 4
EARLY = 128
REST = 256 - EARLY


def place(x, y, z, c):
    x = lax.rem(x + NX, NX)
    y = lax.rem(y + NY, NY)
    z = lax.rem(z + NZ, NZ)
    c = lax.rem(c, 2)
    return ((y * 2 + x // 2) * 2 + c, z * 2 + lax.rem(x, 2))


class Straight:
    def __init__(self, targets, take, put, bufs, send, recv):
        self.targets, self.take, self.put = targets, take, put
        self.bufs, self.send, self.recv = bufs, send, recv

    def first(self, part):
        for i in (1, 0, 2):
            copy = pltpu.make_async_remote_copy(
                src_ref=self.take(part, i + 1), dst_ref=self.bufs.at[part, i], send_sem=self.send,
                recv_sem=self.recv.at[part], device_id=self.targets[i], device_id_type=MESH,
            )
            copy.start()

    def finish(self, part):
        landed(self.bufs.at[part], self.recv.at[part])
        mine = self.take(part, 0)

        def add(k, _):
            total = mine[k].astype(F32)
            for i in range(3):
                total += self.bufs[part, i, k].astype(F32)
            self.put(4 * part + k, total)
            return 0

        lax.fori_loop(0, 4, add, 0)

    def drain(self):
        landed(self.bufs, self.send)


LINE = [(dx, dc) for dx in range(NX) for dc in range(2) if (dx, dc) != (0, 0)]
GROUP = [(dx, dy, dc) for dx in (2, 0) for dy in (2, 1, 3, 0) for dc in (1, 0) if (dx, dy, dc) != (0, 0, 0)]
PARTNERS = sorted(
    set((dx, 0, 0, dc) for dx, dc in LINE)
    | set((0, dy, 0, 0) for dy in range(1, NY))
    | set((0, 0, dz, 0) for dz in range(1, NZ))
    | set((dx, dy, 0, dc) for dx, dy, dc in GROUP)
)


def landed(view, sem):
    pltpu.make_async_copy(view, view, sem).wait()


class Ring:
    def __init__(self, plus, minus, take, put, bufs, send, recv):
        self.plus, self.minus, self.take, self.put = plus, minus, take, put
        self.bufs, self.send, self.recv = bufs, send, recv

    def go(self, src, slot, to):
        copy = pltpu.make_async_remote_copy(
            src_ref=src, dst_ref=self.bufs.at[slot], send_sem=self.send,
            recv_sem=self.recv.at[slot], device_id=to, device_id_type=MESH,
        )
        copy.start()

    def arrived(self, slot):
        landed(self.bufs.at[slot], self.recv.at[slot])

    def first(self, part):
        if part == 0:
            self.go(self.take(0, 2), 0, self.plus)
            self.go(self.take(0, -1), 2, self.minus)
        else:
            self.go(self.take(1, 2), 1, self.minus)
            self.go(self.take(1, 1), 3, self.plus)

    def second(self, part):
        step = 1 if part == 0 else -1
        self.arrived(part)
        mine = self.take(part, step)

        def add(i, _):
            mine[i] = (mine[i].astype(F32) + self.bufs[part, i].astype(F32)).astype(BF16)
            return 0

        lax.fori_loop(0, 4, add, 0)
        self.go(mine, 4 + part, self.plus if part == 0 else self.minus)

    def finish(self, part):
        self.arrived(2 + part)
        self.arrived(4 + part)
        mine = self.take(part, 0)

        def add(i, _):
            total = mine[i].astype(F32) + self.bufs[2 + part, i].astype(F32)
            self.put(4 * part + i, total + self.bufs[4 + part, i].astype(F32))
            return 0

        lax.fori_loop(0, 4, add, 0)

    def drain(self):
        landed(self.bufs, self.send)


def kernel(
    x_hbm, q_hbm, k_hbm, g_hbm, w_hbm,
    value_v, grad_v, peak_out,
    xh, q_v, k_v, g_v, wfull, cot, coded_t,
    part_x, part_y, xbuf, ybuf, fin, r1, r2, r3, r4, zrecv, piece, piece_all,
    other_v, pk, pk1, pk2, pk3, x_out,
    load_sem, xown_sem, xother_sem, xs_sem, xr_sem, wown_sem, ax_s, ax_r, az_s, az_r,
    cot_s, cot_r, p1s, p1r, p2s, p2r, p3s, p3r,
    r1s, r1r, r2s, r2r, r3s, r3r, r4s, r4r, zs, zr, cs, cr, oth_s, oth_r,
):
    rep, fsdp = lax.axis_index("rep"), lax.axis_index("fsdp")
    c = lax.rem(rep, 2)
    xhi = lax.rem(rep // 2, 2)
    y = rep // 4
    xlo = lax.rem(fsdp, 2)
    z = fsdp // 2
    x = 2 * xhi + xlo
    xot = 1 - xlo

    def at(dx=0, dy=0, dz=0, dc=0):
        return place(x + dx, y + dy, z + dz, c + dc)

    mate = at(dc=1)
    barrier = pltpu.get_barrier_semaphore()
    for partner in PARTNERS:
        pl.semaphore_signal(barrier, inc=1, device_id=at(*partner), device_id_type=MESH)

    def half_cols(f, half):
        return x_hbm.at[:, pl.ds(pl.multiple_of(f * 512 + half * 256, 256), 256)]

    def x_own(f):
        return pltpu.make_async_copy(half_cols(f, c), xh.at[f, pl.ds(0, T), :], xown_sem)

    def x_other(f):
        return pltpu.make_async_copy(half_cols(f, 1 - c), x_out.at[f], xother_sem)

    def x_swap(f):
        return pltpu.make_async_remote_copy(
            src_ref=x_out.at[f], dst_ref=xh.at[f, pl.ds(T, T), :], send_sem=xs_sem,
            recv_sem=xr_sem.at[f // 8], device_id=mate, device_id_type=MESH,
        )

    def x_give(f, _):
        x_swap(f).start()
        return 0


    lax.fori_loop(0, 16, lambda f, _: (x_other(f).start(), 0)[1], 0)
    loads = [pltpu.make_async_copy(k_hbm, k_v, load_sem.at[4])]
    for a in range(KV_HEADS):
        cols = pl.ds(a * PER_KV * HEAD, PER_KV * HEAD)
        loads.append(pltpu.make_async_copy(q_hbm.at[:, cols], q_v.at[:, cols], load_sem.at[a]))
        loads.append(pltpu.make_async_copy(g_hbm.at[:, cols], g_v.at[:, cols], load_sem.at[a]))
    w_half = w_hbm.at[pl.ds(pl.multiple_of(c * 256, 256), 256), :]
    w_own = pltpu.make_async_copy(w_half, wfull.at[fsdp], wown_sem)
    for copy in loads[:5]:
        copy.start()
    w_own.start()
    lax.fori_loop(0, 16, lambda f, _: (x_own(f).start(), 0)[1], 0)
    for copy in loads[5:]:
        copy.start()

    key_pos = lax.broadcasted_iota(jnp.int32, (T, 2 * T), 0)
    query_pos = lax.broadcasted_iota(jnp.int32, (T, 2 * T), 1)
    keep = key_pos <= jnp.where(query_pos >= T, query_pos - T, query_pos)

    def attention(a):
        if a == 0:
            loads[0].wait()
        landed(q_v.at[:, pl.ds(0, 2 * PER_KV * HEAD)], load_sem.at[a])
        keys = k_v[:, a * HEAD:(a + 1) * HEAD]
        total = jnp.zeros((T, HEAD), F32)
        for pair in range(PER_KV // 2):
            base = (a * PER_KV + 2 * pair) * HEAD
            qs = jnp.concatenate([q_v[:, base:base + HEAD], q_v[:, base + HEAD:base + 2 * HEAD]], axis=0)
            gs = jnp.concatenate([g_v[:, base:base + HEAD], g_v[:, base + HEAD:base + 2 * HEAD]], axis=0)
            scores = lax.dot_general(
                keys, qs, (((1,), (1,)), ((), ())), preferred_element_type=F32
            ) * (1.0 / math.sqrt(HEAD))
            scores = jnp.where(keep, scores, -jnp.inf)
            expo = jnp.exp(scores - jnp.max(scores, axis=0, keepdims=True))
            prob = (expo * (1.0 / jnp.sum(expo, axis=0, keepdims=True))).astype(BF16)
            total += jnp.dot(prob, gs, preferred_element_type=F32)
        cot[0, :, a * HEAD:(a + 1) * HEAD] = total.astype(BF16)
        return jnp.max(jnp.abs(total), axis=0, keepdims=True)

    top_g = attention(0)
    pl.semaphore_wait(barrier, len(PARTNERS))
    landed(x_out, xother_sem)
    lax.fori_loop(0, 16, x_give, 0)

    def across(b, block, base, count, sem):
        for i, dx in enumerate((1, -1)):
            view = wfull.at[block, pl.ds(base + i * (count // 2), count // 2), :]
            copy = pltpu.make_async_remote_copy(
                src_ref=view, dst_ref=view, send_sem=ax_s.at[sem], recv_sem=ax_r.at[sem],
                device_id=at(dx=dx), device_id_type=MESH,
            )
            copy.start()

    def across_wait(b, k):
        landed(wfull.at[0, pl.ds(0, REST if k else EARLY), :], ax_r.at[8 if k else b])

    def spread(dz):
        across(dz % NZ, lax.rem(z + dz + NZ, NZ) * 2 + xlo, 0, EARLY, dz % NZ)

    WHOLE, LATE = (0, 256), (EARLY, REST)

    def az_list(d, p):
        if d < 4:
            return [(way, WHOLE if p == 0 else LATE) for way in range(2)]
        return [(p, WHOLE)]

    def az_slot(d, p):
        return (d - 1) * 2 + p

    def az_view(d, p):
        if p == 0 and d < 4:
            return wfull.at[pl.ds(0, 2)]
        if p == 1 and d < 4:
            return wfull.at[pl.ds(0, 2), pl.ds(0, REST), :]
        return wfull.at[0]

    def az_send(d, p):
        for way, (base, count) in az_list(d, p):
            dz = 1 - 2 * way
            block = lax.rem(z - dz * (d - 1) + NZ, NZ) * 2 + (xlo if p == 0 else xot)
            slot = az_slot(d, p)
            rows = pl.ds(base, count)
            copy = pltpu.make_async_remote_copy(
                src_ref=wfull.at[block, rows, :], dst_ref=wfull.at[block, rows, :], send_sem=az_s.at[slot], recv_sem=az_r.at[slot],
                device_id=at(dz=dz), device_id_type=MESH,
            )
            copy.start()

    def az_wait(d, p):
        landed(az_view(d, p), az_r.at[az_slot(d, p)])

    cot_copies = []

    def cot_send(s):
        cols = pl.ds(256 * s, 256)
        cot_copies.append(pltpu.make_async_remote_copy(
            src_ref=cot.at[0, :, cols], dst_ref=cot.at[1, :, cols], send_sem=cot_s.at[s], recv_sem=cot_r.at[s],
            device_id=mate, device_id_type=MESH,
        ))
        cot_copies[-1].start()

    def peak_send(stage, targets, got, s_sem, r_sem):
        for i, to in enumerate(targets):
            copy = pltpu.make_async_remote_copy(
                src_ref=pk.at[stage], dst_ref=got.at[i], send_sem=s_sem, recv_sem=r_sem,
                device_id=to, device_id_type=MESH,
            )
            copy.start()

    def peak_join(stage, count, got, r_sem):
        top = pk[stage]
        landed(got, r_sem)
        for i in range(count):
            top = jnp.maximum(top, got[i])
        pk[stage + 1] = top

    def product(s):
        def one(pair, _):
            for k in range(4):
                zd, xl = pair * 2 + k // 2, k % 2
                out = jnp.dot(coded_t[...], xh[zd * 2 + xl], preferred_element_type=F32)
                out = out.astype(BF16).reshape(2, 2, NY, 16, 256)
                part_x[s, xl, :, zd] = out[0]
                for yd in range(NY):
                    part_y[s, yd, zd, xl] = out[1, :, yd]
            return 0
        return one

    def xdest(step):
        xd = lax.rem(x + step + NX, NX)
        return lax.rem(xd, 2), xd // 2

    def ydest(step):
        return lax.rem(y + step + NY, NY)

    xp, xm, yp, ym = at(dx=1), at(dx=-1), at(dy=1), at(dy=-1)

    def rings(s):
        def take1(p, step):
            xl, xg = xdest(step)
            return part_x.at[s, xl, xg, pl.ds(4 * p, 4)]

        def take2(p, step):
            return part_y.at[s, ydest(step), pl.ds(4 * p, 4)]

        def take3(p, step):
            return xbuf.at[s, ydest(step), pl.ds(4 * p, 4)]

        def take4(p, step):
            xl, xg = xdest(step)
            return ybuf.at[s, xl, xg, pl.ds(4 * p, 4)]

        def put1(i, v):
            xbuf[s, :, i] = v.astype(BF16)

        def put2(i, v):
            ybuf[s, :, :, i] = v.astype(BF16)

        def put3(i, v):
            fin[s, i, 0] = v.astype(BF16)

        def put4(i, v):
            fin[s, i, 1] = v.astype(BF16)

        return (
            Ring(xp, xm, take1, put1, r1.at[s], r1s.at[s], r1r.at[s]),
            Ring(yp, ym, take2, put2, r2.at[s], r2s.at[s], r2r.at[s]),
            Straight([at(dy=i) for i in (1, 2, 3)], take3, put3, r3.at[s], r3s.at[s], r3r.at[s]),
            Straight([at(dx=i) for i in (1, 2, 3)], take4, put4, r4.at[s], r4s.at[s], r4r.at[s]),
        )

    stages = [rings(0), rings(1)]

    def start(s):
        cot_copies[s].wait_recv()
        both = cot[:, :, 256 * s:256 * (s + 1)].reshape(2 * T, 256)
        coded_t[...] = jnp.transpose(both.astype(F32)).astype(BF16)
        ra, rb = stages[s][:2]
        if s == 0:
            landed(x_out, xown_sem)
            landed(x_out.at[pl.ds(0, 8)], xr_sem.at[0])
        lax.fori_loop(0, 2, product(s), 0)
        ra.first(0)
        rb.first(0)
        if s == 0:
            landed(x_out.at[pl.ds(0, 8)], xr_sem.at[1])
        lax.fori_loop(2, 4, product(s), 0)
        ra.first(1)
        rb.first(1)

    def second(s):
        ra, rb = stages[s][:2]
        for p in range(2):
            ra.second(p)
            rb.second(p)

    def turn(s):
        for p in range(2):
            for k in range(2):
                stages[s][k].finish(p)
                stages[s][2 + k].first(p)

    def z_send(s):
        for p in range(2):
            for k in range(2):
                stages[s][2 + k].finish(p)
        for i in (4, 3, 5, 2, 6, 1, 7):
            zd = lax.rem(z + i, NZ)
            copy = pltpu.make_async_remote_copy(
                src_ref=fin.at[s, zd], dst_ref=zrecv.at[s, i], send_sem=zs.at[s], recv_sem=zr.at[s],
                device_id=at(dz=i), device_id_type=MESH,
            )
            copy.start()

    j = xhi * NY + y

    def c_send(s):
        total = fin[s, z].astype(F32)
        landed(zrecv.at[s, pl.ds(1, NZ - 1)], zr.at[s])
        for i in range(1, NZ):
            total += zrecv[s, i].astype(F32)
        piece[s] = (total * (1.0 / 256.0)).astype(BF16)
        for dx, dy, dc in GROUP:
            copy = pltpu.make_async_remote_copy(
                src_ref=piece.at[s], dst_ref=piece_all.at[c, pl.ds(2 * s, 2), j], send_sem=cs.at[s],
                recv_sem=cr.at[s], device_id=at(dx=dx, dy=dy, dc=dc), device_id_type=MESH,
            )
            copy.start()
        piece_all[c, pl.ds(2 * s, 2), j] = piece[s]

    def out_cols(f):
        return pl.ds(pl.multiple_of(f * 512 + c * 256, 256), 256)

    def mate_out(f):
        return pltpu.make_async_remote_copy(
            src_ref=other_v.at[f], dst_ref=grad_v.at[:, out_cols(f)],
            send_sem=oth_s, recv_sem=oth_r, device_id=mate, device_id_type=MESH,
        )

    def input_grad(zb):
        zb = lax.rem(zb + NZ, NZ)

        rows = cot[...].reshape(2 * T, KV)
        for xl in range(2):
            f = zb * 2 + xl
            out = lax.dot_general(rows, wfull[f], (((1,), (1,)), ((), ())), preferred_element_type=F32)
            out = out.astype(BF16)
            grad_v[:, out_cols(f)] = out[0:T]
            other_v[f] = out[T:2 * T]
        for xl in range(2):
            mate_out(zb * 2 + xl).start()

    def c_view():
        return wfull.at[0, pl.ds(0, 16 * len(GROUP)), :]

    def v_turn(s):
        landed(c_view(), cr.at[s])
        for half in range(2):
            turned = jnp.transpose(piece_all[half, pl.ds(2 * s, 2)].reshape(256, 256).astype(F32))
            value_v[256 * half:256 * (half + 1), 256 * s:256 * (s + 1)] = turned.astype(BF16)

    def az_sent(d, p):
        landed(az_view(d, p), az_s.at[az_slot(d, p)])

    def across_sent(b):
        landed(wfull.at[0, pl.ds(0, REST if b == 8 else EARLY), :], ax_s.at[b])

    w_own.wait()
    across(0, fsdp, EARLY, REST, 8)
    spread(0)
    az_send(1, 0)
    top_g = jnp.maximum(top_g, attention(1))
    cot_send(0)
    top_g = jnp.maximum(top_g, attention(2))
    top_g = jnp.maximum(top_g, attention(3))
    cot_send(1)
    start(0)
    across_wait(0, 1)
    az_send(1, 1)
    start(1)
    second(0)
    az_wait(1, 0)
    az_send(2, 0)
    top_x = lax.fori_loop(
        0, 16,
        lambda f, top: jnp.maximum(top, jnp.max(jnp.abs(xh[f].astype(F32)), axis=0, keepdims=True)),
        jnp.zeros((1, 256), F32),
    )
    top_w = jnp.max(jnp.abs(wfull[fsdp].astype(F32)), axis=0, keepdims=True)
    row = lax.broadcasted_iota(jnp.int32, (8, 128), 0)
    tops = [jnp.max(top, axis=1, keepdims=True) for top in (top_x, top_w, top_g)]
    pk[0] = jnp.where(row == 0, tops[0], jnp.where(row == 1, tops[1], tops[2]))
    peak_send(0, [at(dx=dx, dc=dc) for dx, dc in LINE], pk1, p1s, p1r)
    second(1)
    az_wait(1, 1)
    az_send(2, 1)
    turn(0)
    across_wait(0, 0)
    input_grad(z)
    az_wait(2, 0)
    az_send(3, 0)
    turn(1)
    spread(1)
    spread(-1)
    peak_join(0, len(LINE), pk1, p1r)
    peak_send(1, [at(dy=dy) for dy in range(1, NY)], pk2, p2s, p2r)
    az_wait(2, 1)
    az_send(3, 1)
    z_send(0)
    z_send(1)
    spread(2)
    spread(-2)
    az_wait(3, 0)
    az_send(4, 0)
    spread(3)
    spread(-3)
    landed(x_out, xs_sem)
    for s in range(2):
        cot_copies[s].wait_send()
        for ring in stages[s][:2]:
            ring.drain()
    for d in (1, 2):
        for p in range(2):
            az_sent(d, p)
    landed(pk1, p1s)
    for dz in (1, -1):
        across_wait(dz % NZ, 0)
        input_grad(z + dz)
    c_send(0)
    az_wait(3, 1)
    across_wait(3, 0)
    az_send(4, 1)
    peak_join(1, NY - 1, pk2, p2r)
    peak_send(2, [at(dz=dz) for dz in range(1, NZ)], pk3, p3s, p3r)
    c_send(1)
    for s in range(2):
        landed(zrecv.at[s, pl.ds(1, NZ - 1)], zs.at[s])
        for ring in stages[s][2:]:
            ring.drain()
    landed(c_view(), cs.at[0])
    landed(pk2, p2s)
    for b in (0, 1, 2, 6, 7, 8):
        across_sent(b)
    for dz in (2, -2):
        across_wait(dz % NZ, 0)
        input_grad(z + dz)
    v_turn(0)
    across_wait(NZ - 3, 0)
    input_grad(z + 3)
    input_grad(z - 3)
    az_sent(3, 0)
    az_sent(3, 1)
    across_sent(3)
    across_sent(5)
    v_turn(1)
    peak_join(2, NZ - 1, pk3, p3r)
    peak_out[...] = pk[3]
    az_wait(4, 0)
    az_wait(4, 1)
    input_grad(z + 4)

    az_sent(4, 0)
    az_sent(4, 1)
    landed(c_view(), cs.at[1])
    landed(pk3, p3s)
    landed(other_v, oth_s)
    landed(other_v, oth_r)


def hand_over(value, grad, peaks, value_out, grad_out, peaks_out, weight_out, sems):
    copies = [pltpu.make_async_copy(value, value_out, sems.at[0])]
    for i in range(CUTS):
        rows = pl.ds(i * (T // CUTS), T // CUTS)
        copies.append(pltpu.make_async_copy(grad.at[rows], grad_out.at[rows], sems.at[1 + i]))
    for copy in copies:
        copy.start()
    peaks_out[0] = jnp.max(peaks[0:1])
    peaks_out[1] = jnp.max(peaks[2:3])
    weight_out[0] = jnp.max(peaks[1:2])
    for copy in copies:
        copy.wait()


def body(layer_input, queries, keys, context_gradient, weight):
    dma = pltpu.SemaphoreType.DMA
    vm = pltpu.VMEM
    anywhere = pl.BlockSpec(memory_space=pl.ANY)
    scalars = pl.BlockSpec(memory_space=pltpu.SMEM)
    value_grad, input_grad, peaks = pl.pallas_call(
        kernel,
        out_shape=(
            vm((512, KV), BF16),
            vm((T, D), BF16),
            vm((8, 128), F32),
        ),
        in_specs=[anywhere] * 5,
        out_specs=(pl.BlockSpec(memory_space=pltpu.VMEM),) * 3,
        scratch_shapes=[
            vm((16, 2 * T, 256), BF16), vm((T, 4096), BF16), vm((T, KV), BF16), vm((T, 4096), BF16),
            vm((16, 256, KV), BF16), vm((2, T, KV), BF16), vm((256, 2 * T), BF16),
            vm((2, 2, 2, NZ, NY, 16, 256), BF16), vm((2, NY, NZ, 2, 2, 16, 256), BF16),
            vm((2, NY, NZ, 16, 256), BF16), vm((2, 2, 2, NZ, 16, 256), BF16), vm((2, NZ, 2, 16, 256), BF16),
            vm((2, 6, 4, NY, 16, 256), BF16), vm((2, 6, 4, 2, 2, 16, 256), BF16),
            vm((2, 2, 3, 4, 16, 256), BF16), vm((2, 2, 3, 4, 16, 256), BF16),
            vm((2, NZ, 2, 16, 256), BF16), vm((2, 2, 16, 256), BF16), vm((2, 4, 8, 16, 256), BF16),
            vm((16, T, 256), BF16),
            vm((4, 8, 128), F32), vm((7, 8, 128), F32), vm((3, 8, 128), F32), vm((7, 8, 128), F32),
            vm((16, T, 256), BF16),
            dma((5,)), dma, dma, dma, dma((2,)), dma, dma((9,)), dma((9,)), dma((8,)), dma((8,)),
            dma((2,)), dma((2,)), dma, dma, dma, dma, dma, dma,
            dma((2,)), dma((2, 6)), dma((2,)), dma((2, 6)), dma((2,)), dma((2, 2)), dma((2,)), dma((2, 2)),
            dma((2,)), dma((2,)), dma((2,)), dma((2,)), dma, dma,
        ],
        compiler_params=pltpu.CompilerParams(
            collective_id=0, has_side_effects=True, vmem_limit_bytes=60 << 20
        ),
        name="value_backward",
    )(layer_input, queries, keys, context_gradient, weight)
    return pl.pallas_call(
        hand_over,
        out_shape=(
            jax.ShapeDtypeStruct((512, KV), BF16),
            jax.ShapeDtypeStruct((T, D), BF16),
            jax.ShapeDtypeStruct((2,), F32),
            jax.ShapeDtypeStruct((1,), F32),
        ),
        in_specs=[pl.BlockSpec(memory_space=pltpu.VMEM)] * 3,
        out_specs=(anywhere, anywhere, scalars, scalars),
        scratch_shapes=[dma((1 + CUTS,))],
        compiler_params=pltpu.CompilerParams(vmem_limit_bytes=1 << 20),
        name="hand_over",
    )(value_grad, input_grad, peaks)


def solution(mesh):
    return jax.shard_map(
        body,
        mesh=mesh,
        in_specs=(
            P(("rep", "fsdp"), None),
            P(("rep", "fsdp"), None),
            P(("rep", "fsdp"), None),
            P(("rep", "fsdp"), None),
            P("fsdp", None),
        ),
        out_specs=(P("fsdp", None), P(("rep", "fsdp"), None), P(), P()),
        check_vma=False,
    )
```

```python
import functools
import math

import jax
import jax.numpy as jnp
from jax import lax
from jax.experimental import pallas as pl
from jax.experimental.pallas import tpu as pltpu
from jax.sharding import PartitionSpec as P

HEAD = 128
QUERY_HEADS = 32
KV_HEADS = 4
PER_KV = QUERY_HEADS // KV_HEADS
T = 192
D = 8192
KV = KV_HEADS * HEAD
MESH = pl.DeviceIdType.MESH
F32 = jnp.float32
BF16 = jnp.bfloat16
NX, NY, NZ = 4, 4, 8
CUTS = 4
EARLY = 128
REST = 256 - EARLY


def place(x, y, z, c):
    x = lax.rem(x + NX, NX)
    y = lax.rem(y + NY, NY)
    z = lax.rem(z + NZ, NZ)
    c = lax.rem(c, 2)
    return ((y * 2 + x // 2) * 2 + c, z * 2 + lax.rem(x, 2))


class Straight:
    def __init__(self, targets, take, put, bufs, send, recv):
        self.targets, self.take, self.put = targets, take, put
        self.bufs, self.send, self.recv = bufs, send, recv

    def first(self, part):
        for i in (1, 0, 2):
            copy = pltpu.make_async_remote_copy(
                src_ref=self.take(part, i + 1), dst_ref=self.bufs.at[part, i], send_sem=self.send,
                recv_sem=self.recv.at[part], device_id=self.targets[i], device_id_type=MESH,
            )
            copy.start()

    def finish(self, part):
        landed(self.bufs.at[part], self.recv.at[part])
        mine = self.take(part, 0)

        def add(k, _):
            total = mine[k].astype(F32)
            for i in range(3):
                total += self.bufs[part, i, k].astype(F32)
            self.put(4 * part + k, total)
            return 0

        lax.fori_loop(0, 4, add, 0)


LINE = [(dx, dc) for dx in range(NX) for dc in range(2) if (dx, dc) != (0, 0)]
GROUP = [(dx, dy, dc) for dx in (2, 0) for dy in (2, 1, 3, 0) for dc in (1, 0) if (dx, dy, dc) != (0, 0, 0)]
PARTNERS = sorted(
    set((dx, 0, 0, dc) for dx, dc in LINE)
    | set((0, dy, 0, 0) for dy in range(1, NY))
    | set((0, 0, dz, 0) for dz in range(1, NZ))
    | set((dx, dy, 0, dc) for dx, dy, dc in GROUP)
)


def landed(view, sem):
    pltpu.make_async_copy(view, view, sem).wait()


class Ring:
    def __init__(self, plus, minus, take, put, bufs, send, recv):
        self.plus, self.minus, self.take, self.put = plus, minus, take, put
        self.bufs, self.send, self.recv = bufs, send, recv

    def go(self, src, slot, to):
        copy = pltpu.make_async_remote_copy(
            src_ref=src, dst_ref=self.bufs.at[slot], send_sem=self.send,
            recv_sem=self.recv.at[slot], device_id=to, device_id_type=MESH,
        )
        copy.start()

    def arrived(self, slot):
        landed(self.bufs.at[slot], self.recv.at[slot])

    def first(self, part):
        if part == 0:
            self.go(self.take(0, 2), 0, self.plus)
            self.go(self.take(0, -1), 2, self.minus)
        else:
            self.go(self.take(1, 2), 1, self.minus)
            self.go(self.take(1, 1), 3, self.plus)

    def second(self, part):
        step = 1 if part == 0 else -1
        self.arrived(part)
        mine = self.take(part, step)

        def add(i, _):
            mine[i] = (mine[i].astype(F32) + self.bufs[part, i].astype(F32)).astype(BF16)
            return 0

        lax.fori_loop(0, 4, add, 0)
        self.go(mine, 4 + part, self.plus if part == 0 else self.minus)

    def finish(self, part):
        self.arrived(2 + part)
        self.arrived(4 + part)
        mine = self.take(part, 0)

        def add(i, _):
            total = mine[i].astype(F32) + self.bufs[2 + part, i].astype(F32)
            self.put(4 * part + i, total + self.bufs[4 + part, i].astype(F32))
            return 0

        lax.fori_loop(0, 4, add, 0)


def kernel(
    x_hbm, q_hbm, k_hbm, g_hbm, w_hbm,
    value_v, grad_v, peak_out,
    xh, q_v, k_v, g_v, wfull, cot, coded_t,
    part_x, part_y, xbuf, ybuf, fin, r1, r2, r3, r4, zrecv, piece, piece_all,
    other_v, pk, pk1, pk2, pk3, x_out,
    load_sem, xown_sem, xother_sem, xs_sem, xr_sem, wown_sem, ax_s, ax_r, az_s, az_r,
    cot_s, cot_r, p1s, p1r, p2s, p2r, p3s, p3r,
    r1s, r1r, r2s, r2r, r3s, r3r, r4s, r4r, zs, zr, cs, cr, oth_s, oth_r,
):
    rep, fsdp = lax.axis_index("rep"), lax.axis_index("fsdp")
    c = lax.rem(rep, 2)
    xhi = lax.rem(rep // 2, 2)
    y = rep // 4
    xlo = lax.rem(fsdp, 2)
    z = fsdp // 2
    x = 2 * xhi + xlo
    xot = 1 - xlo

    def at(dx=0, dy=0, dz=0, dc=0):
        return place(x + dx, y + dy, z + dz, c + dc)

    mate = at(dc=1)
    barrier = pltpu.get_barrier_semaphore()
    for partner in PARTNERS:
        pl.semaphore_signal(barrier, inc=1, device_id=at(*partner), device_id_type=MESH)

    def half_cols(f, half):
        return x_hbm.at[:, pl.ds(pl.multiple_of(f * 512 + half * 256, 256), 256)]

    def x_own(f):
        return pltpu.make_async_copy(half_cols(f, c), xh.at[f, pl.ds(0, T), :], xown_sem)

    def x_other(f):
        return pltpu.make_async_copy(half_cols(f, 1 - c), x_out.at[f], xother_sem)

    def x_swap(f):
        return pltpu.make_async_remote_copy(
            src_ref=x_out.at[f], dst_ref=xh.at[f, pl.ds(T, T), :], send_sem=xs_sem,
            recv_sem=xr_sem.at[f // 8], device_id=mate, device_id_type=MESH,
        )

    def x_give(f, _):
        x_swap(f).start()
        return 0


    lax.fori_loop(0, 16, lambda f, _: (x_other(f).start(), 0)[1], 0)
    loads = [pltpu.make_async_copy(k_hbm, k_v, load_sem.at[4])]
    for a in range(KV_HEADS):
        cols = pl.ds(a * PER_KV * HEAD, PER_KV * HEAD)
        loads.append(pltpu.make_async_copy(q_hbm.at[:, cols], q_v.at[:, cols], load_sem.at[a]))
        loads.append(pltpu.make_async_copy(g_hbm.at[:, cols], g_v.at[:, cols], load_sem.at[a]))
    w_half = w_hbm.at[pl.ds(pl.multiple_of(c * 256, 256), 256), :]
    w_own = pltpu.make_async_copy(w_half, wfull.at[fsdp], wown_sem)
    for copy in loads[:5]:
        copy.start()
    w_own.start()
    lax.fori_loop(0, 16, lambda f, _: (x_own(f).start(), 0)[1], 0)
    for copy in loads[5:]:
        copy.start()

    key_pos = lax.broadcasted_iota(jnp.int32, (T, 2 * T), 0)
    query_pos = lax.broadcasted_iota(jnp.int32, (T, 2 * T), 1)
    keep = key_pos <= jnp.where(query_pos >= T, query_pos - T, query_pos)

    def attention(a):
        if a == 0:
            loads[0].wait()
        landed(q_v.at[:, pl.ds(0, 2 * PER_KV * HEAD)], load_sem.at[a])
        keys = k_v[:, a * HEAD:(a + 1) * HEAD]
        total = jnp.zeros((T, HEAD), F32)
        for pair in range(PER_KV // 2):
            base = (a * PER_KV + 2 * pair) * HEAD
            qs = jnp.concatenate([q_v[:, base:base + HEAD], q_v[:, base + HEAD:base + 2 * HEAD]], axis=0)
            gs = jnp.concatenate([g_v[:, base:base + HEAD], g_v[:, base + HEAD:base + 2 * HEAD]], axis=0)
            scores = lax.dot_general(
                keys, qs, (((1,), (1,)), ((), ())), preferred_element_type=F32
            ) * (1.0 / math.sqrt(HEAD))
            scores = jnp.where(keep, scores, -jnp.inf)
            expo = jnp.exp(scores - jnp.max(scores, axis=0, keepdims=True))
            prob = (expo * (1.0 / jnp.sum(expo, axis=0, keepdims=True))).astype(BF16)
            total += jnp.dot(prob, gs, preferred_element_type=F32)
        cot[0, :, a * HEAD:(a + 1) * HEAD] = total.astype(BF16)
        return jnp.max(jnp.abs(total), axis=0, keepdims=True)

    top_g = attention(0)
    pl.semaphore_wait(barrier, len(PARTNERS))
    landed(x_out, xother_sem)
    lax.fori_loop(0, 16, x_give, 0)

    def across(b, block, base, count, sem):
        for i, dx in enumerate((1, -1)):
            view = wfull.at[block, pl.ds(base + i * (count // 2), count // 2), :]
            copy = pltpu.make_async_remote_copy(
                src_ref=view, dst_ref=view, send_sem=ax_s, recv_sem=ax_r.at[sem],
                device_id=at(dx=dx), device_id_type=MESH,
            )
            copy.start()

    def across_wait(b, k):
        landed(wfull.at[0, pl.ds(0, REST if k else EARLY), :], ax_r.at[8 if k else b])

    def spread(dz):
        across(dz % NZ, lax.rem(z + dz + NZ, NZ) * 2 + xlo, 0, EARLY, dz % NZ)

    WHOLE, LATE = (0, 256), (EARLY, REST)

    def az_list(d, p):
        if d < 4:
            return [(way, WHOLE if p == 0 else LATE) for way in range(2)]
        return [(p, WHOLE)]

    def az_slot(d, p):
        return (d - 1) * 2 + p

    def az_view(d, p):
        if p == 0 and d < 4:
            return wfull.at[pl.ds(0, 2)]
        if p == 1 and d < 4:
            return wfull.at[pl.ds(0, 2), pl.ds(0, REST), :]
        return wfull.at[0]

    def az_send(d, p):
        for way, (base, count) in az_list(d, p):
            dz = 1 - 2 * way
            block = lax.rem(z - dz * (d - 1) + NZ, NZ) * 2 + (xlo if p == 0 else xot)
            slot = az_slot(d, p)
            rows = pl.ds(base, count)
            copy = pltpu.make_async_remote_copy(
                src_ref=wfull.at[block, rows, :], dst_ref=wfull.at[block, rows, :], send_sem=az_s, recv_sem=az_r.at[slot],
                device_id=at(dz=dz), device_id_type=MESH,
            )
            copy.start()

    def az_wait(d, p):
        landed(az_view(d, p), az_r.at[az_slot(d, p)])

    cot_copies = []

    def cot_send(s):
        cols = pl.ds(256 * s, 256)
        cot_copies.append(pltpu.make_async_remote_copy(
            src_ref=cot.at[0, :, cols], dst_ref=cot.at[1, :, cols], send_sem=cot_s, recv_sem=cot_r.at[s],
            device_id=mate, device_id_type=MESH,
        ))
        cot_copies[-1].start()

    def peak_send(stage, targets, got, s_sem, r_sem):
        for i, to in enumerate(targets):
            copy = pltpu.make_async_remote_copy(
                src_ref=pk.at[stage], dst_ref=got.at[i], send_sem=s_sem, recv_sem=r_sem,
                device_id=to, device_id_type=MESH,
            )
            copy.start()

    def peak_join(stage, count, got, r_sem):
        top = pk[stage]
        landed(got, r_sem)
        for i in range(count):
            top = jnp.maximum(top, got[i])
        pk[stage + 1] = top

    def product(s):
        def one(pair, _):
            for k in range(4):
                zd, xl = pair * 2 + k // 2, k % 2
                out = jnp.dot(coded_t[...], xh[zd * 2 + xl], preferred_element_type=F32)
                out = out.astype(BF16).reshape(2, 2, NY, 16, 256)
                part_x[s, xl, :, zd] = out[0]
                for yd in range(NY):
                    part_y[s, yd, zd, xl] = out[1, :, yd]
            return 0
        return one

    def xdest(step):
        xd = lax.rem(x + step + NX, NX)
        return lax.rem(xd, 2), xd // 2

    def ydest(step):
        return lax.rem(y + step + NY, NY)

    xp, xm, yp, ym = at(dx=1), at(dx=-1), at(dy=1), at(dy=-1)

    def rings(s):
        def take1(p, step):
            xl, xg = xdest(step)
            return part_x.at[s, xl, xg, pl.ds(4 * p, 4)]

        def take2(p, step):
            return part_y.at[s, ydest(step), pl.ds(4 * p, 4)]

        def take3(p, step):
            return xbuf.at[s, ydest(step), pl.ds(4 * p, 4)]

        def take4(p, step):
            xl, xg = xdest(step)
            return ybuf.at[s, xl, xg, pl.ds(4 * p, 4)]

        def put1(i, v):
            xbuf[s, :, i] = v.astype(BF16)

        def put2(i, v):
            ybuf[s, :, :, i] = v.astype(BF16)

        def put3(i, v):
            fin[s, i, 0] = v.astype(BF16)

        def put4(i, v):
            fin[s, i, 1] = v.astype(BF16)

        return (
            Ring(xp, xm, take1, put1, r1.at[s], r1s, r1r.at[s]),
            Ring(yp, ym, take2, put2, r2.at[s], r2s, r2r.at[s]),
            Straight([at(dy=i) for i in (1, 2, 3)], take3, put3, r3.at[s], r3s, r3r.at[s]),
            Straight([at(dx=i) for i in (1, 2, 3)], take4, put4, r4.at[s], r4s, r4r.at[s]),
        )

    stages = [rings(0), rings(1)]

    def start(s):
        cot_copies[s].wait_recv()
        both = cot[:, :, 256 * s:256 * (s + 1)].reshape(2 * T, 256)
        coded_t[...] = jnp.transpose(both.astype(F32)).astype(BF16)
        ra, rb = stages[s][:2]
        if s == 0:
            landed(x_out, xown_sem)
            landed(x_out.at[pl.ds(0, 8)], xr_sem.at[0])
        lax.fori_loop(0, 2, product(s), 0)
        ra.first(0)
        rb.first(0)
        if s == 0:
            landed(x_out.at[pl.ds(0, 8)], xr_sem.at[1])
        lax.fori_loop(2, 4, product(s), 0)
        ra.first(1)
        rb.first(1)

    def second(s):
        ra, rb = stages[s][:2]
        for p in range(2):
            ra.second(p)
            rb.second(p)

    def turn(s):
        for p in range(2):
            for k in range(2):
                stages[s][k].finish(p)
                stages[s][2 + k].first(p)

    def z_send(s):
        for p in range(2):
            for k in range(2):
                stages[s][2 + k].finish(p)
        for i in (4, 3, 5, 2, 6, 1, 7):
            zd = lax.rem(z + i, NZ)
            copy = pltpu.make_async_remote_copy(
                src_ref=fin.at[s, zd], dst_ref=zrecv.at[s, i], send_sem=zs, recv_sem=zr.at[s],
                device_id=at(dz=i), device_id_type=MESH,
            )
            copy.start()

    j = xhi * NY + y

    def c_send(s):
        total = fin[s, z].astype(F32)
        landed(zrecv.at[s, pl.ds(1, NZ - 1)], zr.at[s])
        for i in range(1, NZ):
            total += zrecv[s, i].astype(F32)
        piece[s] = (total * (1.0 / 256.0)).astype(BF16)
        for dx, dy, dc in GROUP:
            copy = pltpu.make_async_remote_copy(
                src_ref=piece.at[s], dst_ref=piece_all.at[c, pl.ds(2 * s, 2), j], send_sem=cs,
                recv_sem=cr.at[s], device_id=at(dx=dx, dy=dy, dc=dc), device_id_type=MESH,
            )
            copy.start()
        piece_all[c, pl.ds(2 * s, 2), j] = piece[s]

    def out_cols(f):
        return pl.ds(pl.multiple_of(f * 512 + c * 256, 256), 256)

    def mate_out(f):
        return pltpu.make_async_remote_copy(
            src_ref=other_v.at[f], dst_ref=grad_v.at[:, out_cols(f)],
            send_sem=oth_s, recv_sem=oth_r, device_id=mate, device_id_type=MESH,
        )

    def input_grad(zb):
        zb = lax.rem(zb + NZ, NZ)

        rows = cot[...].reshape(2 * T, KV)
        for xl in range(2):
            f = zb * 2 + xl
            out = lax.dot_general(rows, wfull[f], (((1,), (1,)), ((), ())), preferred_element_type=F32)
            out = out.astype(BF16)
            grad_v[:, out_cols(f)] = out[0:T]
            other_v[f] = out[T:2 * T]
        for xl in range(2):
            mate_out(zb * 2 + xl).start()

    def c_view():
        return wfull.at[0, pl.ds(0, 16 * len(GROUP)), :]

    def v_turn(s):
        landed(c_view(), cr.at[s])
        for half in range(2):
            turned = jnp.transpose(piece_all[half, pl.ds(2 * s, 2)].reshape(256, 256).astype(F32))
            value_v[256 * half:256 * (half + 1), 256 * s:256 * (s + 1)] = turned.astype(BF16)

    w_own.wait()
    across(0, fsdp, EARLY, REST, 8)
    spread(0)
    az_send(1, 0)
    top_g = jnp.maximum(top_g, attention(1))
    cot_send(0)
    top_g = jnp.maximum(top_g, attention(2))
    top_g = jnp.maximum(top_g, attention(3))
    cot_send(1)
    start(0)
    across_wait(0, 1)
    az_send(1, 1)
    start(1)
    second(0)
    az_wait(1, 0)
    az_send(2, 0)
    top_x = lax.fori_loop(
        0, 16,
        lambda f, top: jnp.maximum(top, jnp.max(jnp.abs(xh[f].astype(F32)), axis=0, keepdims=True)),
        jnp.zeros((1, 256), F32),
    )
    top_w = jnp.max(jnp.abs(wfull[fsdp].astype(F32)), axis=0, keepdims=True)
    row = lax.broadcasted_iota(jnp.int32, (8, 128), 0)
    tops = [jnp.max(top, axis=1, keepdims=True) for top in (top_x, top_w, top_g)]
    pk[0] = jnp.where(row == 0, tops[0], jnp.where(row == 1, tops[1], tops[2]))
    peak_send(0, [at(dx=dx, dc=dc) for dx, dc in LINE], pk1, p1s, p1r)
    second(1)
    az_wait(1, 1)
    az_send(2, 1)
    turn(0)
    across_wait(0, 0)
    input_grad(z)
    az_wait(2, 0)
    az_send(3, 0)
    turn(1)
    spread(1)
    spread(-1)
    peak_join(0, len(LINE), pk1, p1r)
    peak_send(1, [at(dy=dy) for dy in range(1, NY)], pk2, p2s, p2r)
    az_wait(2, 1)
    az_send(3, 1)
    z_send(0)
    z_send(1)
    spread(2)
    spread(-2)
    az_wait(3, 0)
    az_send(4, 0)
    spread(3)
    spread(-3)
    landed(x_out, xs_sem)
    landed(pk1, p1s)
    for dz in (1, -1):
        across_wait(dz % NZ, 0)
        input_grad(z + dz)
    c_send(0)
    az_wait(3, 1)
    across_wait(3, 0)
    az_send(4, 1)
    peak_join(1, NY - 1, pk2, p2r)
    peak_send(2, [at(dz=dz) for dz in range(1, NZ)], pk3, p3s, p3r)
    c_send(1)
    landed(pk2, p2s)
    for dz in (2, -2):
        across_wait(dz % NZ, 0)
        input_grad(z + dz)
    v_turn(0)
    across_wait(NZ - 3, 0)
    input_grad(z + 3)
    input_grad(z - 3)
    v_turn(1)
    peak_join(2, NZ - 1, pk3, p3r)
    peak_out[...] = pk[3]
    az_wait(4, 0)
    az_wait(4, 1)
    input_grad(z + 4)

    landed(wfull.at[pl.ds(0, 11)], az_s)
    landed(wfull.at[pl.ds(0, 4)], ax_s)
    landed(cot.at[0], cot_s)
    for bufs, sem in ((r1, r1s), (r2, r2s), (r3, r3s), (r4, r4s)):
        landed(bufs, sem)
    landed(zrecv.at[:, pl.ds(1, NZ - 1)], zs)
    landed(wfull.at[pl.ds(0, 2), pl.ds(0, 16 * len(GROUP)), :], cs)
    landed(pk3, p3s)
    landed(other_v, oth_s)
    landed(other_v, oth_r)


def hand_over(value, grad, peaks, value_out, grad_out, peaks_out, weight_out, sems):
    copies = [pltpu.make_async_copy(value, value_out, sems.at[0])]
    for i in range(CUTS):
        rows = pl.ds(i * (T // CUTS), T // CUTS)
        copies.append(pltpu.make_async_copy(grad.at[rows], grad_out.at[rows], sems.at[1 + i]))
    for copy in copies:
        copy.start()
    peaks_out[0] = jnp.max(peaks[0:1])
    peaks_out[1] = jnp.max(peaks[2:3])
    weight_out[0] = jnp.max(peaks[1:2])
    for copy in copies:
        copy.wait()


def body(layer_input, queries, keys, context_gradient, weight):
    dma = pltpu.SemaphoreType.DMA
    vm = pltpu.VMEM
    anywhere = pl.BlockSpec(memory_space=pl.ANY)
    scalars = pl.BlockSpec(memory_space=pltpu.SMEM)
    value_grad, input_grad, peaks = pl.pallas_call(
        kernel,
        out_shape=(
            vm((512, KV), BF16),
            vm((T, D), BF16),
            vm((8, 128), F32),
        ),
        in_specs=[anywhere] * 5,
        out_specs=(pl.BlockSpec(memory_space=pltpu.VMEM),) * 3,
        scratch_shapes=[
            vm((16, 2 * T, 256), BF16), vm((T, 4096), BF16), vm((T, KV), BF16), vm((T, 4096), BF16),
            vm((16, 256, KV), BF16), vm((2, T, KV), BF16), vm((256, 2 * T), BF16),
            vm((2, 2, 2, NZ, NY, 16, 256), BF16), vm((2, NY, NZ, 2, 2, 16, 256), BF16),
            vm((2, NY, NZ, 16, 256), BF16), vm((2, 2, 2, NZ, 16, 256), BF16), vm((2, NZ, 2, 16, 256), BF16),
            vm((2, 6, 4, NY, 16, 256), BF16), vm((2, 6, 4, 2, 2, 16, 256), BF16),
            vm((2, 2, 3, 4, 16, 256), BF16), vm((2, 2, 3, 4, 16, 256), BF16),
            vm((2, NZ, 2, 16, 256), BF16), vm((2, 2, 16, 256), BF16), vm((2, 4, 8, 16, 256), BF16),
            vm((16, T, 256), BF16),
            vm((4, 8, 128), F32), vm((7, 8, 128), F32), vm((3, 8, 128), F32), vm((7, 8, 128), F32),
            vm((16, T, 256), BF16),
            dma((5,)), dma, dma, dma, dma((2,)), dma, dma, dma((9,)), dma, dma((8,)),
            dma, dma((2,)), dma, dma, dma, dma, dma, dma,
            dma, dma((2, 6)), dma, dma((2, 6)), dma, dma((2, 2)), dma, dma((2, 2)),
            dma, dma((2,)), dma, dma((2,)), dma, dma,
        ],
        compiler_params=pltpu.CompilerParams(
            collective_id=0, has_side_effects=True, vmem_limit_bytes=60 << 20
        ),
        name="value_backward",
    )(layer_input, queries, keys, context_gradient, weight)
    return pl.pallas_call(
        hand_over,
        out_shape=(
            jax.ShapeDtypeStruct((512, KV), BF16),
            jax.ShapeDtypeStruct((T, D), BF16),
            jax.ShapeDtypeStruct((2,), F32),
            jax.ShapeDtypeStruct((1,), F32),
        ),
        in_specs=[pl.BlockSpec(memory_space=pltpu.VMEM)] * 3,
        out_specs=(anywhere, anywhere, scalars, scalars),
        scratch_shapes=[dma((1 + CUTS,))],
        compiler_params=pltpu.CompilerParams(vmem_limit_bytes=1 << 20),
        name="hand_over",
    )(value_grad, input_grad, peaks)


def solution(mesh):
    return jax.shard_map(
        body,
        mesh=mesh,
        in_specs=(
            P(("rep", "fsdp"), None),
            P(("rep", "fsdp"), None),
            P(("rep", "fsdp"), None),
            P(("rep", "fsdp"), None),
            P("fsdp", None),
        ),
        out_specs=(P("fsdp", None), P(("rep", "fsdp"), None), P(), P()),
        check_vma=False,
    )
```
